128 devices in a mesh: row: 8 (over y_hi, x), col: 16 (over y_lo, z, core).
Axes of the slice: x: 4, y: 4 (y_hi: 2, y_lo: 2; y = y_hi * 2 + y_lo), z: 4, core: 2. Of those that a mesh axis runs over, the one named last changes fastest.
Arguments:
- pair: bfloat16 [768, 768, 128], P('row', 'col'), may hold values from -6 to 6
- atoms: bfloat16 [24576, 128], P(('row', 'col')), may hold values from -6 to 6
- token_atoms: int32 [768], replicated, may hold values from 16 to 48, as said below
- pair_gain: float32 [128], replicated, may hold values from 0.1 to 1.9
- tri_proj: bfloat16 [128, 640], replicated, may hold values from -0.5 to 0.5
- tri_out: bfloat16 [128, 128], replicated, may hold values from -0.5 to 0.5
- out_gain: float32 [128], replicated, may hold values from 0.1 to 1.9
- bias_weight: float32 [128, 4], replicated, may hold values from -30 to 30
- atom_gain: float32 [128], replicated, may hold values from 0.1 to 1.9
- atom_proj: bfloat16 [128, 512], replicated, may hold values from -0.5 to 0.5
- atom_out: bfloat16 [128, 128], replicated, may hold values from -0.5 to 0.5
- trans_gain: float32 [128], replicated, may hold values from 0.1 to 1.9
- trans_up: bfloat16 [128, 512], replicated, may hold values from -0.5 to 0.5
- trans_down: bfloat16 [256, 128], replicated, may hold values from -0.375 to 0.375
Outputs:
- pair_out: bfloat16 [768, 768, 128], P('row', 'col')
- atoms_out: bfloat16 [24576, 128], P(('row', 'col'))
The draws below stay inside these ranges and needn't reach their ends.
Inputs may be any that keep to these rules, and one draw needn't show every extreme that they name: `token_atoms`: every aligned block of 96 tokens holds exactly 3072 atoms in all.
All inputs are finite; a program needn't handle non-finite values.
Results may differ from the reference program's by a relative error of at most 0.012.
Values may be sent and summed in bfloat16 or wider, within the bound.
No kernel may reach another device: no remote copies, remote signals or barrier semaphores. Data moves between devices by JAX's collectives and lax.ppermute only.
A program may use at most 192 MiB of HBM per device.

```python
import math
import jax
import jax.numpy as jnp
from jax import lax

PAIR_C = 128
TRI_H = 128
ATOM_C = 128
HEADS = 4
HEAD_DIM = 32
TRANS_H = 256
TOK_ROWS = 96
ATOMS_TOK = 32
QUERIES = 32
KEYS = 128
HALO = 48
TOKENS = 768
ATOMS = 24576


def draw_token_atoms(key, part):
    key = jax.random.fold_in(key, 11)
    key_spread, key_order = jax.random.split(key)
    half_span = ATOMS_TOK // 2
    spread = jax.random.randint(key_spread, (TOKENS // TOK_ROWS, TOK_ROWS // 2), -half_span, half_span + 1)
    spread = spread.at[0, 0].set(half_span)
    counts = jnp.concatenate([ATOMS_TOK + spread, ATOMS_TOK - spread], axis=1)
    scores = jax.random.randint(key_order, (TOKENS // TOK_ROWS, TOK_ROWS), 0, 1 << 20) * TOK_ROWS + jnp.arange(TOK_ROWS)[None, :]
    ordering = jnp.argsort(scores, axis=1)
    counts = jnp.take_along_axis(counts, ordering, axis=1)
    return counts.reshape(TOKENS).astype(jnp.int32)


def draw_bias_weight(key, part):
    key = jax.random.fold_in(key, 23)
    values = jax.random.normal(key, (PAIR_C, HEADS), jnp.float32)
    values = jnp.clip(values, -4.0, 4.0) / math.sqrt(PAIR_C)
    return values


def shard_levels(key, shape, cuts, smallest, high):
    level, own = 1.0, jax.random.fold_in(key, 6)
    for position, parts in cuts:
        draws = jnp.exp(jax.random.uniform(jax.random.fold_in(own, position), (parts,), jnp.float32, smallest / len(cuts), high / len(cuts)))
        level = level * jnp.repeat(draws, shape[position] // parts).reshape([-1 if axis == position else 1 for axis in range(len(shape))])
    return level


def centred(key, dims, deviation, bound, cuts=(), kind=jnp.bfloat16):
    array = jax.random.normal(key, dims, jnp.float32) * deviation
    if len(cuts) > 0:
        array = shard_levels(key, dims, cuts, -0.22, 0.18) * array
    return jnp.clip(array, min=-bound, max=bound).astype(kind)


def setup_inputs(seed: int = 0) -> dict:
    key_of = jax.random.split(jax.random.key(seed), 15)
    pair = centred(key_of[0], (TOKENS, TOKENS, PAIR_C), 1.0, 6.0, ((0, 8), (1, 16)))
    atoms = centred(key_of[1], (ATOMS, ATOM_C), 1.0, 6.0, ((0, 128),))
    token_atoms = draw_token_atoms(jax.random.fold_in(key_of[14], 71), 0)
    pair_gain = jnp.clip(1.0 + 0.18 * jax.random.normal(key_of[3], (PAIR_C,), jnp.float32), 0.1, 1.9)
    tri_proj = centred(key_of[4], (PAIR_C, 4 * TRI_H + PAIR_C), PAIR_C ** -0.5, 0.5)
    tri_out = centred(key_of[5], (TRI_H, PAIR_C), TRI_H ** -0.5, 0.5)
    out_gain = jnp.clip(1.0 + 0.18 * jax.random.normal(key_of[6], (TRI_H,), jnp.float32), 0.1, 1.9)
    bias_weight = draw_bias_weight(jax.random.fold_in(key_of[14], 71), 0)
    atom_gain = jnp.clip(1.0 + 0.18 * jax.random.normal(key_of[8], (ATOM_C,), jnp.float32), 0.1, 1.9)
    atom_proj = centred(key_of[9], (ATOM_C, 4 * ATOM_C), ATOM_C ** -0.5, 0.5)
    atom_out = centred(key_of[10], (ATOM_C, ATOM_C), ATOM_C ** -0.5, 0.5)
    trans_gain = jnp.clip(1.0 + 0.18 * jax.random.normal(key_of[11], (ATOM_C,), jnp.float32), 0.1, 1.9)
    trans_up = centred(key_of[12], (ATOM_C, 2 * TRANS_H), ATOM_C ** -0.5, 0.5)
    trans_down = centred(key_of[13], (TRANS_H, ATOM_C), TRANS_H ** -0.5, 0.375)
    return dict(pair=pair, atoms=atoms, token_atoms=token_atoms, pair_gain=pair_gain, tri_proj=tri_proj, tri_out=tri_out, out_gain=out_gain, bias_weight=bias_weight, atom_gain=atom_gain, atom_proj=atom_proj, atom_out=atom_out, trans_gain=trans_gain, trans_up=trans_up, trans_down=trans_down)


EPSILON = 1e-05
HIGHEST = lax.Precision.HIGHEST

def layer_norm(values):
    center = values - lax.optimization_barrier(jnp.mean(values, -1, keepdims=True))
    return center * lax.rsqrt(lax.optimization_barrier(jnp.mean(center * center, -1, keepdims=True)) + EPSILON)

def pair_terms(pair_rows, pair_gain, tri_proj, bias_weight):
    normed = layer_norm(pair_rows.astype(jnp.float32))
    tri_input = (normed * pair_gain).astype(jnp.bfloat16)
    project = jnp.einsum('ijc,cd->ijd', tri_input.astype(jnp.float32), tri_proj.astype(jnp.float32), precision=HIGHEST)
    left_edge = (jax.nn.sigmoid(project[..., :TRI_H]) * project[..., TRI_H:2 * TRI_H]).astype(jnp.bfloat16)
    right_edge = (jax.nn.sigmoid(project[..., 2 * TRI_H:3 * TRI_H]) * project[..., 3 * TRI_H:4 * TRI_H]).astype(jnp.bfloat16)
    out_gate = jax.nn.sigmoid(project[..., 4 * TRI_H:])
    token_bias = jnp.einsum('ijc,ch->ijh', normed, bias_weight, precision=HIGHEST)
    return (left_edge, right_edge, out_gate, token_bias)

def reference(pair, atoms, token_atoms, pair_gain, tri_proj, tri_out, out_gain, bias_weight, atom_gain, atom_proj, atom_out, trans_gain, trans_up, trans_down):
    blocks = TOKENS // TOK_ROWS
    pieces = lax.map(lambda rows_blk: pair_terms(rows_blk, pair_gain, tri_proj, bias_weight), pair.reshape(blocks, TOK_ROWS, TOKENS, PAIR_C))
    left_all, right_all, gate_all, bias_all = [member.reshape((TOKENS, TOKENS) + member.shape[3:]) for member in pieces]
    right_wide = right_all.astype(jnp.float32)

    def update_rows(inputs):
        left_rows, gate_rows, pair_rows = inputs
        product = jnp.einsum('ikc,jkc->ijc', left_rows.astype(jnp.float32), right_wide, precision=HIGHEST)
        tri_normed = (layer_norm(product) * out_gain).astype(jnp.bfloat16)
        update = jnp.einsum('ijc,cd->ijd', tri_normed.astype(jnp.float32), tri_out.astype(jnp.float32), precision=HIGHEST)
        return (pair_rows.astype(jnp.float32) + gate_rows * update).astype(jnp.bfloat16)
    pair_out = lax.map(update_rows, (left_all.reshape(blocks, TOK_ROWS, TOKENS, TRI_H), gate_all.reshape(blocks, TOK_ROWS, TOKENS, PAIR_C), pair.reshape(blocks, TOK_ROWS, TOKENS, PAIR_C))).reshape(TOKENS, TOKENS, PAIR_C)
    atom_total = TOKENS * ATOMS_TOK
    token_ends = jnp.cumsum(token_atoms).astype(jnp.int32)
    atom_index = jnp.arange(atom_total, dtype=jnp.int32)
    token_of = jnp.searchsorted(token_ends, atom_index, side='right').astype(jnp.int32)
    atom_input = (layer_norm(atoms.astype(jnp.float32)) * atom_gain).astype(jnp.bfloat16)
    project = jnp.dot(atom_input, atom_proj, preferred_element_type=jnp.float32).astype(jnp.bfloat16)
    windows = atom_total // QUERIES
    padded = jnp.pad(project[:, ATOM_C:3 * ATOM_C], ((HALO, HALO), (0, 0)))
    key_pos = QUERIES * jnp.arange(windows, dtype=jnp.int32)[:, None] + jnp.arange(KEYS, dtype=jnp.int32)[None, :]
    key_rows = padded[key_pos]
    key_global = key_pos - HALO
    key_valid = (key_global >= 0) & (key_global < atom_total)
    key_token = token_of[jnp.clip(key_global, 0, atom_total - 1)]
    query_token = token_of.reshape(windows, QUERIES)
    pair_bias = bias_all[query_token[:, :, None], key_token[:, None, :]]
    query_rows = project[:, :ATOM_C].reshape(windows, QUERIES, HEADS, HEAD_DIM).astype(jnp.float32)
    key_part = key_rows[..., :ATOM_C].reshape(windows, KEYS, HEADS, HEAD_DIM).astype(jnp.float32)
    value_part = key_rows[..., ATOM_C:].reshape(windows, KEYS, HEADS, HEAD_DIM).astype(jnp.float32)
    score_scale = HEAD_DIM ** (-0.5)
    scores = jnp.einsum('bqhd,bkhd->bhqk', query_rows, key_part, precision=HIGHEST) * score_scale + pair_bias.transpose(0, 3, 1, 2)
    scores = jnp.where(key_valid[:, None, None, :], scores, -jnp.inf)
    row_max = lax.optimization_barrier(jnp.max(scores, -1, keepdims=True))
    exp_scores = jnp.exp(scores - row_max)
    weights = (exp_scores / lax.optimization_barrier(jnp.sum(exp_scores, -1, keepdims=True))).astype(jnp.bfloat16)
    mixed_heads = jnp.einsum('bhqk,bkhd->bqhd', weights.astype(jnp.float32), value_part, precision=HIGHEST)
    gate_value = jax.nn.sigmoid(project[:, 3 * ATOM_C:].astype(jnp.float32)).reshape(windows, QUERIES, HEADS, HEAD_DIM)
    attended = (mixed_heads * gate_value).reshape(atom_total, ATOM_C).astype(jnp.bfloat16)
    atom_state = atoms.astype(jnp.float32) + jnp.dot(attended, atom_out, preferred_element_type=jnp.float32)
    trans_input = (layer_norm(atom_state) * trans_gain).astype(jnp.bfloat16)
    upward = jnp.dot(trans_input, trans_up, preferred_element_type=jnp.float32)
    activated = (jax.nn.silu(upward[:, :TRANS_H]) * upward[:, TRANS_H:]).astype(jnp.bfloat16)
    atoms_out = (atom_state + jnp.dot(activated, trans_down, preferred_element_type=jnp.float32)).astype(jnp.bfloat16)
    return (pair_out, atoms_out)
```

```python
import functools

import jax
import jax.numpy as jnp
from jax import lax
from jax.experimental import pallas as pl
from jax.experimental.pallas import tpu as pltpu
from jax.sharding import PartitionSpec as P

ROWS = 96
COLS = 48
LANES = 128
CHANNELS = 128
TOKENS = 768
QUERIES = 32
KEYS = 128
HALO = 48
ATOM_ROWS = 192
KEY_ROWS = ATOM_ROWS + 2 * HALO
HEADS = 4
HEAD_DIM = 32
NEAR = 5
BAND_ROWS = 16
BAND_COLS = 32
EDGE_ROWS = 72
SUM_ROWS = 40
EPSILON = 1e-05
BOTH = ("row", "col")
VMEM_LIMIT = 56 * 1024 * 1024

F32 = jnp.float32
BF16 = jnp.bfloat16


def layer_norm(values):
    center = values - jnp.mean(values, -1, keepdims=True)
    return center * lax.rsqrt(jnp.mean(center * center, -1, keepdims=True) + EPSILON)


def sigmoid(values):
    return 0.5 * jnp.tanh(0.5 * values) + 0.5


def edges_kernel(pair_ref, gain_ref, weight_ref, edges_ref, normed_ref, stage_ref):
    gain = gain_ref[...]
    weight = weight_ref[...]

    def norm_step(step, carry):
        tile = pair_ref[pl.ds(step * 8, 8)].astype(F32).reshape(8 * COLS, CHANNELS)
        normed_ref[pl.ds(pl.multiple_of(step * 8 * COLS, 8 * COLS), 8 * COLS), :] = (
            layer_norm(tile) * gain
        )
        return carry

    lax.fori_loop(0, ROWS // 8, norm_step, 0)

    def packed(col, third, extra):
        main = normed_ref[pl.ds(col, ROWS, stride=COLS), :]
        rest = normed_ref[pl.ds(third * 32 * COLS + extra, 32, stride=COLS), :]
        return jnp.concatenate([main, rest], 0).astype(BF16)

    def emit(sources, left_at, right_at):
        for at in range(0, len(sources), 2):
            rows = jnp.concatenate([packed(*source) for source in sources[at : at + 2]], 0)
            project = lax.dot_general(
                weight, rows, (((1,), (1,)), ((), ())), preferred_element_type=F32
            )
            left = sigmoid(project[:128]) * project[128:256]
            right = sigmoid(project[256:384]) * project[384:]
            for half in range(2):
                lanes = slice(half * LANES, (half + 1) * LANES)
                stage_ref[pl.ds(left_at + at + half, CHANNELS, stride=16), :] = left[:, lanes]
                stage_ref[pl.ds(right_at + at + half, CHANNELS, stride=16), :] = right[:, lanes]

    def block(group, carry):
        sources = []
        for at in range(8):
            third = jnp.where(group < 3, group, at // 4)
            extra = jnp.where(group < 3, 36 + at, 44 + at % 4)
            sources.append((group * 8 + at, third, extra))
        emit(sources, 0, 8)
        edges_ref[:, pl.ds(pl.multiple_of(group * 16, 16), 16), :] = (
            stage_ref[...].reshape(CHANNELS, 16, LANES).astype(BF16)
        )
        return carry

    lax.fori_loop(0, 4, block, 0)
    emit([(32 + at, 2, 44 + at) for at in range(4)], 0, 4)
    edges_ref[:, 64:72, :] = stage_ref[...].reshape(CHANNELS, 16, LANES)[:, :8].astype(BF16)


def edges(pair, pair_gain, weight):
    return pl.pallas_call(
        edges_kernel,
        out_shape=jax.ShapeDtypeStruct((CHANNELS, EDGE_ROWS, LANES), BF16),
        scratch_shapes=[
            pltpu.VMEM((ROWS * COLS, CHANNELS), F32),
            pltpu.VMEM((CHANNELS * 16, LANES), F32),
        ],
        compiler_params=pltpu.CompilerParams(vmem_limit_bytes=VMEM_LIMIT),
        cost_estimate=pl.CostEstimate(
            flops=2 * ROWS * COLS * 128 * 512, bytes_accessed=4000000, transcendentals=1200000
        ),
        name="edges",
    )(pair, pair_gain, weight)


def triangle_kernel(chunks_ref, sums_ref, left_ref, right_ref, flip_ref, out_ref):
    lane = lax.broadcasted_iota(jnp.int32, (8, LANES), 1)
    low = lax.broadcasted_iota(jnp.int32, (8, LANES), 0) < 4

    def thirds(first, second, third):
        return jnp.where(
            lane < 32,
            pltpu.roll(first, 32, 1),
            jnp.where(lane < 64, pltpu.roll(second, 64, 1), pltpu.roll(third, 96, 1)),
        )

    for row in range(8):

        def gather(col, carry):
            chunk = chunks_ref[row * 16 + col].astype(F32)
            part = [chunk[at * 8 : at * 8 + 8] for at in range(9)]
            tail = part[8]
            turned = pltpu.roll(tail, 4, 0)
            at_rows = pl.ds(pl.multiple_of(col * COLS, COLS), COLS)
            left, right = part[0:8:2], part[1:8:2]
            for ref, main, last, spare in (
                (left_ref, left, tail, turned),
                (right_ref, right, turned, tail),
            ):
                fine = thirds(pltpu.roll(main[3], 4, 0), main[3], spare)
                whole = jnp.concatenate(
                    main + [thirds(main[0], main[1], main[2]), jnp.where(low, last, fine)], 0
                )
                ref[at_rows, row * LANES : (row + 1) * LANES] = whole.astype(BF16)
            return carry

        lax.fori_loop(0, 16, gather, 0)
        flip_ref[row * LANES : (row + 1) * LANES, :] = right_ref[
            :, row * LANES : (row + 1) * LANES
        ].T

    for pair_at in range(4):
        out_ref[...] = jnp.dot(
            flip_ref[...],
            left_ref[:, pair_at * 256 : (pair_at + 1) * 256],
            preferred_element_type=F32,
        )
        for half in range(2):
            row = pair_at * 2 + half

            def pack(col_pair, carry):
                for side in range(2):
                    start = pl.multiple_of(col_pair * LANES + side * COLS, 16)
                    block = out_ref[pl.ds(start, COLS), half * LANES : (half + 1) * LANES]
                    rest = block[40:48]
                    head = [
                        jnp.where(
                            lane < 96, block[at * 8 : at * 8 + 8], pltpu.roll(rest, 96 - 32 * at, 1)
                        )
                        for at in range(3)
                    ]
                    whole = jnp.concatenate(head + [block[24:40]], 0)
                    sums_ref[row * 16 + col_pair * 2 + side] = whole.astype(BF16)
                return carry

            lax.fori_loop(0, 8, pack, 0)


def triangle(chunks):
    return pl.pallas_call(
        triangle_kernel,
        out_shape=jax.ShapeDtypeStruct((CHANNELS, SUM_ROWS, LANES), BF16),
        scratch_shapes=[
            pltpu.VMEM((TOKENS, 1024), BF16),
            pltpu.VMEM((TOKENS, 1024), BF16),
            pltpu.VMEM((1024, TOKENS), BF16),
            pltpu.VMEM((1024, 256), F32),
        ],
        compiler_params=pltpu.CompilerParams(vmem_limit_bytes=VMEM_LIMIT),
        cost_estimate=pl.CostEstimate(
            flops=2 * 1024 * 1024 * 768, bytes_accessed=4000000, transcendentals=0
        ),
        name="triangle",
    )(chunks)


def update_kernel(sums_ref, pair_ref, gate_ref, gain_ref, weight_ref, out_ref, normed_ref, update_ref):
    gain = gain_ref[...]
    weight = weight_ref[...]

    def norm_step(step, carry):
        rows = pl.ds(pl.multiple_of(step * 8, 8), 8)
        tile = sums_ref[:, rows, :].astype(F32)
        center = tile - jnp.mean(tile, 0, keepdims=True)
        scale = lax.rsqrt(jnp.mean(center * center, 0, keepdims=True) + EPSILON)
        normed_ref[...] = (center * scale).reshape(CHANNELS * 8, LANES)
        for at in range(8):
            block = (normed_ref[pl.ds(at, CHANNELS, stride=8), :] * gain).astype(BF16)
            update = lax.dot_general(
                block, weight, (((0,), (0,)), ((), ())), preferred_element_type=F32
            )
            update_ref[pl.ds(step * 8 + at, ROWS, stride=COLS), :] = update[:ROWS]

            @pl.when(step < 3)
            def _():
                start = step * 32 * COLS + 40 + at
                update_ref[pl.ds(start, 32, stride=COLS), :] = update[ROWS:]

        return carry

    lax.fori_loop(0, SUM_ROWS // 8, norm_step, 0)

    def out_step(step, carry):
        rows = pl.ds(step * 8, 8)
        update = update_ref[pl.ds(pl.multiple_of(step * 8 * COLS, 8 * COLS), 8 * COLS), :]
        update = update.reshape(8, COLS, CHANNELS)
        out_ref[rows] = (pair_ref[rows].astype(F32) + gate_ref[rows] * update).astype(BF16)
        return carry

    lax.fori_loop(0, ROWS // 8, out_step, 0)


def update_pair(sums, pair, gate, out_gain, tri_out):
    return pl.pallas_call(
        update_kernel,
        out_shape=jax.ShapeDtypeStruct((ROWS, COLS, CHANNELS), BF16),
        scratch_shapes=[
            pltpu.VMEM((CHANNELS * 8, LANES), F32),
            pltpu.VMEM((ROWS * COLS, CHANNELS), F32),
        ],
        compiler_params=pltpu.CompilerParams(vmem_limit_bytes=VMEM_LIMIT),
        cost_estimate=pl.CostEstimate(
            flops=2 * ROWS * COLS * 128 * 128, bytes_accessed=6000000, transcendentals=5000
        ),
        name="update_pair",
    )(sums, pair, gate, out_gain, tri_out)


def split3(values):
    high = values.astype(BF16)
    rest = values - high.astype(F32)
    middle = rest.astype(BF16)
    low = (rest - middle.astype(F32)).astype(BF16)
    return high, middle, low


def side_kernel(
    first_ref, place_ref, pair_ref, gain_ref, weight_ref, bias_ref, gate_ref, band_ref, table_ref
):
    gain = gain_ref[...]
    weight = weight_ref[...]
    bias = jnp.concatenate([part.astype(F32) for part in split3(bias_ref[...])], 0).astype(BF16)
    table_ref[...] = jnp.zeros_like(table_ref)

    def norm_step(step, carry):
        tile = pair_ref[pl.ds(step * 8, 8)].astype(F32).reshape(8 * COLS, CHANNELS)
        normed = layer_norm(tile)
        inputs = (normed * gain).astype(BF16)
        gate = sigmoid(jnp.dot(inputs, weight, preferred_element_type=F32))
        gate_ref[pl.ds(step * 8, 8)] = gate.reshape(8, COLS, CHANNELS)
        parts = split3(normed)
        for at in range(8):
            rows = slice(at * COLS, (at + 1) * COLS)
            found = sum(
                lax.dot_general(
                    bias, part[rows], (((1,), (1,)), ((), ())), preferred_element_type=F32
                )
                for part in parts
            )
            found = found[0:8] + found[8:16] + found[16:24]
            for head in range(HEADS):
                table_ref[head, pl.ds(8 + step * 8 + at, 1), 0:COLS] = found[head : head + 1]
        return carry

    lax.fori_loop(0, ROWS // 8, norm_step, 0)

    lane = lax.broadcasted_iota(jnp.int32, (BAND_ROWS, LANES), 1)
    row_base = place_ref[0]
    col_base = place_ref[1]

    def band_step(target, carry):
        first = first_ref[target]
        start = first - row_base + 8
        total = jnp.zeros((BAND_ROWS, LANES), F32)
        shift = col_base - (first - NEAR)
        for head in range(HEADS):
            rows = table_ref[head, pl.ds(start, BAND_ROWS), :]
            moved = pltpu.roll(rows, lax.rem(shift + head * BAND_COLS + 16 * LANES, LANES), 1)
            col = lane - head * BAND_COLS - shift
            keep = (lane // BAND_COLS == head) & (col >= 0) & (col < COLS)
            total = total + jnp.where(keep, moved, 0.0)
        band_ref[target] = total
        return carry

    lax.fori_loop(0, 16, band_step, 0)


def side(first, place, pair, pair_gain, gate_weight, bias_wide):
    whole = pl.BlockSpec(memory_space=pltpu.VMEM)
    scalars = pl.BlockSpec(memory_space=pltpu.SMEM)
    return pl.pallas_call(
        side_kernel,
        out_shape=(
            jax.ShapeDtypeStruct((ROWS, COLS, CHANNELS), F32),
            jax.ShapeDtypeStruct((16, BAND_ROWS, LANES), F32),
        ),
        in_specs=[scalars, scalars, whole, whole, whole, whole],
        out_specs=(whole, whole),
        scratch_shapes=[pltpu.VMEM((HEADS, ROWS + 32, LANES), F32)],
        compiler_params=pltpu.CompilerParams(vmem_limit_bytes=VMEM_LIMIT),
        cost_estimate=pl.CostEstimate(
            flops=8 * ROWS * COLS * 128 * 128, bytes_accessed=5000000, transcendentals=600000
        ),
        name="side",
    )(first, place, pair, pair_gain, gate_weight, bias_wide)


def atoms_kernel(
    base_ref,
    atoms_ref,
    before_ref,
    after_ref,
    band_ref,
    lane_start_ref,
    lane_end_ref,
    sub_start_ref,
    sub_end_ref,
    gain_ref,
    project_ref,
    output_ref,
    trans_gain_ref,
    up_ref,
    down_ref,
    out_ref,
):
    base = base_ref[0]
    own = atoms_ref[...].astype(F32)
    around = jnp.concatenate(
        [before_ref[...].astype(F32), own, after_ref[...].astype(F32)], 0
    )
    inputs = (layer_norm(around) * gain_ref[...]).astype(BF16)
    projected = jnp.dot(inputs, project_ref[...], preferred_element_type=F32)
    query = projected[HALO : HALO + ATOM_ROWS, 0:128].astype(BF16)
    key = projected[:, 128:256].astype(BF16)
    value = projected[:, 256:384].astype(BF16)
    gate = projected[HALO : HALO + ATOM_ROWS, 384:512].astype(BF16).astype(F32)

    query_atom = base + lax.broadcasted_iota(jnp.int32, (ATOM_ROWS, LANES), 0)
    query_hot = (
        ((query_atom >= lane_start_ref[...]) & (query_atom < lane_end_ref[...]))
        .astype(F32)
        .astype(BF16)
    )
    key_atom = base - HALO + lax.broadcasted_iota(jnp.int32, (LANES, KEY_ROWS), 1)
    key_hot = (
        ((key_atom >= sub_start_ref[...]) & (key_atom < sub_end_ref[...])).astype(F32)
    )
    token_head = lax.broadcasted_iota(jnp.int32, (LANES, KEY_ROWS), 0) // BAND_COLS

    band = jnp.sum(band_ref[...], 0)
    band = jnp.concatenate([band, jnp.zeros((LANES - BAND_ROWS, LANES), F32)], 0)
    picked = [
        jnp.dot(query_hot, part, preferred_element_type=F32).astype(BF16) for part in split3(band)
    ]

    window = lax.broadcasted_iota(jnp.int32, (ATOM_ROWS, KEY_ROWS), 0) // QUERIES
    place = lax.broadcasted_iota(jnp.int32, (ATOM_ROWS, KEY_ROWS), 1)
    near = place - window * QUERIES
    atom = base - HALO + place
    allowed = (near >= 0) & (near < KEYS) & (atom >= 0) & (atom < TOKENS * 32)
    lane_head = lax.broadcasted_iota(jnp.int32, (ATOM_ROWS, LANES), 1) // HEAD_DIM
    mixed = jnp.zeros((ATOM_ROWS, LANES), F32)
    for head in range(HEADS):
        own_query = jnp.where(lane_head == head, query.astype(F32), 0.0).astype(BF16)
        scores = lax.dot_general(
            own_query, key, (((1,), (1,)), ((), ())), preferred_element_type=F32
        ) * (HEAD_DIM**-0.5)
        head_hot = jnp.where(token_head == head, key_hot, 0.0).astype(BF16)
        for part in picked:
            scores = scores + jnp.dot(part, head_hot, preferred_element_type=F32)
        scores = jnp.where(allowed, scores, -jnp.inf)
        grown = jnp.exp(scores - jnp.max(scores, -1, keepdims=True))
        weights = (grown / jnp.sum(grown, -1, keepdims=True)).astype(BF16)
        mixed = mixed + jnp.where(
            lane_head == head, jnp.dot(weights, value, preferred_element_type=F32), 0.0
        )
    attended = (mixed * sigmoid(gate)).astype(BF16)
    state = own + jnp.dot(attended, output_ref[...], preferred_element_type=F32)
    inner = (layer_norm(state) * trans_gain_ref[...]).astype(BF16)
    upward = jnp.dot(inner, up_ref[...], preferred_element_type=F32)
    first, second = upward[:, :256], upward[:, 256:]
    hidden = (first * sigmoid(first) * second).astype(BF16)
    out_ref[...] = (
        state + jnp.dot(hidden, down_ref[...], preferred_element_type=F32)
    ).astype(BF16)


def atoms_block(base, *arrays):
    whole = pl.BlockSpec(memory_space=pltpu.VMEM)
    return pl.pallas_call(
        atoms_kernel,
        out_shape=jax.ShapeDtypeStruct((ATOM_ROWS, LANES), BF16),
        in_specs=[pl.BlockSpec(memory_space=pltpu.SMEM)] + [whole] * len(arrays),
        out_specs=whole,
        compiler_params=pltpu.CompilerParams(vmem_limit_bytes=VMEM_LIMIT),
        cost_estimate=pl.CostEstimate(
            flops=2 * 400 * 1000 * 1000, bytes_accessed=2000000, transcendentals=400000
        ),
        name="atoms_block",
    )(base, *arrays)


def on_device(
    pair,
    atoms,
    token_atoms,
    pair_gain,
    tri_proj,
    tri_out,
    out_gain,
    bias_weight,
    atom_gain,
    atom_proj,
    atom_out,
    trans_gain,
    trans_up,
    trans_down,
):
    row_id = lax.axis_index("row")
    col_id = lax.axis_index("col")
    device = row_id * 16 + col_id

    weight = tri_proj[:, :512].T
    chunks = edges(pair, pair_gain[None], weight)
    arrived = lax.all_to_all(chunks, BOTH, 0, 0, tiled=True)

    ends = jnp.cumsum(token_atoms)
    starts = ends - token_atoms
    firsts_at = (row_id * 16 + jnp.arange(16, dtype=jnp.int32)) * ATOM_ROWS
    firsts = jnp.sum((ends[None, :] <= firsts_at[:, None]).astype(jnp.int32), 1)
    first = jnp.sum((ends <= device * ATOM_ROWS).astype(jnp.int32))
    far = jnp.full((LANES,), -1, jnp.int32)
    all_starts = jnp.concatenate([far, starts, far])
    all_ends = jnp.concatenate([far, ends, far])
    lane_start = lax.dynamic_slice(all_starts, (first + LANES,), (LANES,))
    lane_end = lax.dynamic_slice(all_ends, (first + LANES,), (LANES,))
    sub_start = lax.dynamic_slice(all_starts, (first + LANES - NEAR,), (BAND_COLS,))
    sub_end = lax.dynamic_slice(all_ends, (first + LANES - NEAR,), (BAND_COLS,))

    bias_wide = jnp.pad(bias_weight.T, ((0, 4), (0, 0)))
    place = jnp.stack([row_id * ROWS, col_id * COLS]).astype(jnp.int32)
    gate, bands = side(firsts, place, pair, pair_gain[None], tri_proj[:, 512:], bias_wide)
    band = lax.all_to_all(bands, "col", 0, 0, tiled=True)

    ring = list(range(127))
    before = lax.ppermute(atoms[ATOM_ROWS - HALO :], BOTH, [(at, at + 1) for at in ring])
    after = lax.ppermute(atoms[:HALO], BOTH, [(at + 1, at) for at in ring])
    atoms_out = atoms_block(
        (device * ATOM_ROWS).astype(jnp.int32)[None],
        atoms,
        before,
        after,
        band,
        lane_start[None],
        lane_end[None],
        jnp.tile(sub_start, HEADS)[:, None],
        jnp.tile(sub_end, HEADS)[:, None],
        atom_gain[None],
        atom_proj,
        atom_out,
        trans_gain[None],
        trans_up,
        trans_down,
    )

    sums = triangle(arrived)
    returned = lax.all_to_all(sums, BOTH, 0, 0, tiled=True)
    pair_out = update_pair(returned, pair, gate, out_gain[:, None], tri_out)
    return (pair_out, atoms_out)


def solution(mesh):
    return jax.shard_map(
        on_device,
        mesh=mesh,
        in_specs=(P("row", "col", None), P(BOTH, None)) + (P(),) * 12,
        out_specs=(P("row", "col", None), P(BOTH, None)),
        check_vma=False,
    )
```

```python
import functools

import jax
import jax.numpy as jnp
from jax import lax
from jax.experimental import pallas as pl
from jax.experimental.pallas import tpu as pltpu
from jax.sharding import PartitionSpec as P

ROWS = 96
COLS = 48
LANES = 128
CHANNELS = 128
TOKENS = 768
QUERIES = 32
KEYS = 128
HALO = 48
ATOM_ROWS = 192
KEY_ROWS = ATOM_ROWS + 2 * HALO
HEADS = 4
HEAD_DIM = 32
NEAR = 5
BAND_ROWS = 16
BAND_COLS = 32
EDGE_ROWS = 72
SUM_ROWS = 40
EPSILON = 1e-05
BOTH = ("row", "col")
VMEM_LIMIT = 20 * 1024 * 1024

F32 = jnp.float32
BF16 = jnp.bfloat16


def layer_norm(values):
    center = values - jnp.mean(values, -1, keepdims=True)
    return center * lax.rsqrt(jnp.mean(center * center, -1, keepdims=True) + EPSILON)


def sigmoid(values):
    return 0.5 * jnp.tanh(0.5 * values) + 0.5


def edges_kernel(pair_ref, gain_ref, weight_ref, edges_ref, gain_out_ref, normed_ref, stage_ref):
    gain = gain_ref[...]
    gain_out_ref[...] = gain
    weight = weight_ref[:, :512].T

    def norm_step(step, carry):
        tile = pair_ref[pl.ds(step * 8, 8)].astype(F32).reshape(8 * COLS, CHANNELS)
        normed_ref[pl.ds(pl.multiple_of(step * 8 * COLS, 8 * COLS), 8 * COLS), :] = (
            layer_norm(tile) * gain
        )
        return carry

    lax.fori_loop(0, ROWS // 8, norm_step, 0, unroll=4)

    def packed(col, third, extra):
        main = normed_ref[pl.ds(col, ROWS, stride=COLS), :]
        rest = normed_ref[pl.ds(third * 32 * COLS + extra, 32, stride=COLS), :]
        return jnp.concatenate([main, rest], 0).astype(BF16)

    def emit(sources, left_at, right_at):
        for at in range(0, len(sources), 2):
            rows = jnp.concatenate([packed(*source) for source in sources[at : at + 2]], 0)
            project = lax.dot_general(
                weight, rows, (((1,), (1,)), ((), ())), preferred_element_type=F32
            )
            left = sigmoid(project[:128]) * project[128:256]
            right = sigmoid(project[256:384]) * project[384:]
            for half in range(2):
                lanes = slice(half * LANES, (half + 1) * LANES)
                stage_ref[pl.ds(left_at + at + half, CHANNELS, stride=16), :] = left[:, lanes]
                stage_ref[pl.ds(right_at + at + half, CHANNELS, stride=16), :] = right[:, lanes]

    def block(group, carry):
        sources = []
        for at in range(8):
            third = jnp.where(group < 3, group, at // 4)
            extra = jnp.where(group < 3, 36 + at, 44 + at % 4)
            sources.append((group * 8 + at, third, extra))
        emit(sources, 0, 8)
        edges_ref[:, pl.ds(pl.multiple_of(group * 16, 16), 16), :] = (
            stage_ref[...].reshape(CHANNELS, 16, LANES).astype(BF16)
        )
        return carry

    lax.fori_loop(0, 4, block, 0, unroll=True)
    emit([(32 + at, 2, 44 + at) for at in range(4)], 0, 4)
    edges_ref[:, 64:72, :] = stage_ref[...].reshape(CHANNELS, 16, LANES)[:, :8].astype(BF16)


def edges(pair, pair_gain, weight):
    return pl.pallas_call(
        edges_kernel,
        out_shape=(
            jax.ShapeDtypeStruct((CHANNELS, EDGE_ROWS, LANES), BF16),
            jax.ShapeDtypeStruct((1, CHANNELS), F32),
        ),
        scratch_shapes=[
            pltpu.VMEM((ROWS * COLS, CHANNELS), F32),
            pltpu.VMEM((CHANNELS * 16, LANES), F32),
        ],
        compiler_params=pltpu.CompilerParams(vmem_limit_bytes=VMEM_LIMIT),
        cost_estimate=pl.CostEstimate(
            flops=2 * ROWS * COLS * 128 * 512, bytes_accessed=4000000, transcendentals=1200000
        ),
        name="edges",
    )(pair, pair_gain, weight)


def triangle_kernel(chunks_ref, sums_ref, left_ref, right_ref, flip_ref, out_ref):
    lane = lax.broadcasted_iota(jnp.int32, (8, LANES), 1)
    low = lax.broadcasted_iota(jnp.int32, (8, LANES), 0) < 4

    def thirds(first, second, third):
        return jnp.where(
            lane < 32,
            pltpu.roll(first, 32, 1),
            jnp.where(lane < 64, pltpu.roll(second, 64, 1), pltpu.roll(third, 96, 1)),
        )

    for row in range(8):

        def gather(col, carry):
            chunk = chunks_ref[row * 16 + col].astype(F32)
            part = [chunk[at * 8 : at * 8 + 8] for at in range(9)]
            tail = part[8]
            turned = pltpu.roll(tail, 4, 0)
            at_rows = pl.ds(pl.multiple_of(col * COLS, COLS), COLS)
            left, right = part[0:8:2], part[1:8:2]
            for ref, main, last, spare in (
                (left_ref, left, tail, turned),
                (right_ref, right, turned, tail),
            ):
                fine = thirds(pltpu.roll(main[3], 4, 0), main[3], spare)
                whole = jnp.concatenate(
                    main + [thirds(main[0], main[1], main[2]), jnp.where(low, last, fine)], 0
                )
                ref[at_rows, row * LANES : (row + 1) * LANES] = whole.astype(BF16)
            return carry

        lax.fori_loop(0, 16, gather, 0, unroll=True)
        flip_ref[row * LANES : (row + 1) * LANES, :] = right_ref[
            :, row * LANES : (row + 1) * LANES
        ].T

    for pair_at in range(4):
        out_ref[...] = jnp.dot(
            flip_ref[...],
            left_ref[:, pair_at * 256 : (pair_at + 1) * 256],
            preferred_element_type=F32,
        )
        for half in range(2):
            row = pair_at * 2 + half

            def pack(col_pair, carry):
                for side in range(2):
                    start = pl.multiple_of(col_pair * LANES + side * COLS, 16)
                    block = out_ref[pl.ds(start, COLS), half * LANES : (half + 1) * LANES]
                    rest = block[40:48]
                    head = [
                        jnp.where(
                            lane < 96, block[at * 8 : at * 8 + 8], pltpu.roll(rest, 96 - 32 * at, 1)
                        )
                        for at in range(3)
                    ]
                    whole = jnp.concatenate(head + [block[24:40]], 0)
                    sums_ref[row * 16 + col_pair * 2 + side] = whole.astype(BF16)
                return carry

            lax.fori_loop(0, 8, pack, 0, unroll=True)


def triangle(chunks):
    return pl.pallas_call(
        triangle_kernel,
        out_shape=jax.ShapeDtypeStruct((CHANNELS, SUM_ROWS, LANES), BF16),
        scratch_shapes=[
            pltpu.VMEM((TOKENS, 1024), BF16),
            pltpu.VMEM((TOKENS, 1024), BF16),
            pltpu.VMEM((1024, TOKENS), BF16),
            pltpu.VMEM((1024, 256), F32),
        ],
        compiler_params=pltpu.CompilerParams(vmem_limit_bytes=VMEM_LIMIT),
        cost_estimate=pl.CostEstimate(
            flops=2 * 1024 * 1024 * 768, bytes_accessed=4000000, transcendentals=0
        ),
        name="triangle",
    )(chunks)


def update_kernel(sums_ref, pair_ref, gate_ref, gain_ref, weight_ref, out_ref, normed_ref, update_ref):
    gain = jnp.broadcast_to(gain_ref[...], (CHANNELS, LANES)).T
    weight = weight_ref[...]

    def norm_step(step, carry):
        rows = pl.ds(pl.multiple_of(step * 8, 8), 8)
        tile = sums_ref[:, rows, :].astype(F32)
        center = tile - jnp.mean(tile, 0, keepdims=True)
        scale = lax.rsqrt(jnp.mean(center * center, 0, keepdims=True) + EPSILON)
        normed_ref[...] = (center * scale).reshape(CHANNELS * 8, LANES)
        for at in range(8):
            block = (normed_ref[pl.ds(at, CHANNELS, stride=8), :] * gain).astype(BF16)
            update = lax.dot_general(
                block, weight, (((0,), (0,)), ((), ())), preferred_element_type=F32
            )
            update_ref[pl.ds(step * 8 + at, ROWS, stride=COLS), :] = update[:ROWS]

            @pl.when(step < 3)
            def _():
                start = step * 32 * COLS + 40 + at
                update_ref[pl.ds(start, 32, stride=COLS), :] = update[ROWS:]

        return carry

    lax.fori_loop(0, SUM_ROWS // 8, norm_step, 0, unroll=True)

    def out_step(step, carry):
        rows = pl.ds(step * 8, 8)
        update = update_ref[pl.ds(pl.multiple_of(step * 8 * COLS, 8 * COLS), 8 * COLS), :]
        update = update.reshape(8, COLS, CHANNELS)
        out_ref[rows] = (pair_ref[rows].astype(F32) + gate_ref[rows] * update).astype(BF16)
        return carry

    lax.fori_loop(0, ROWS // 8, out_step, 0, unroll=4)


def update_pair(sums, pair, gate, out_gain, tri_out):
    return pl.pallas_call(
        update_kernel,
        out_shape=jax.ShapeDtypeStruct((ROWS, COLS, CHANNELS), BF16),
        scratch_shapes=[
            pltpu.VMEM((CHANNELS * 8, LANES), F32),
            pltpu.VMEM((ROWS * COLS, CHANNELS), F32),
        ],
        compiler_params=pltpu.CompilerParams(vmem_limit_bytes=VMEM_LIMIT),
        cost_estimate=pl.CostEstimate(
            flops=2 * ROWS * COLS * 128 * 128, bytes_accessed=6000000, transcendentals=5000
        ),
        name="update_pair",
    )(sums, pair, gate, out_gain, tri_out)


def split3(values):
    high = values.astype(BF16)
    rest = values - high.astype(F32)
    middle = rest.astype(BF16)
    low = (rest - middle.astype(F32)).astype(BF16)
    return high, middle, low


def side_kernel(
    first_ref, place_ref, pair_ref, gain_ref, weight_ref, bias_ref, gate_ref, band_ref, table_ref
):
    gain = gain_ref[...]
    weight = weight_ref[:, 512:]
    bias = jnp.concatenate([part.astype(F32) for part in split3(bias_ref[...])], 0).astype(BF16)
    table_ref[...] = jnp.zeros_like(table_ref)

    def norm_step(step, carry):
        tile = pair_ref[pl.ds(step * 8, 8)].astype(F32).reshape(8 * COLS, CHANNELS)
        normed = layer_norm(tile)
        inputs = (normed * gain).astype(BF16)
        gate = sigmoid(jnp.dot(inputs, weight, preferred_element_type=F32))
        gate_ref[pl.ds(step * 8, 8)] = gate.reshape(8, COLS, CHANNELS)
        parts = split3(normed)
        for at in range(8):
            rows = slice(at * COLS, (at + 1) * COLS)
            found = sum(
                lax.dot_general(
                    bias, part[rows], (((1,), (1,)), ((), ())), preferred_element_type=F32
                )
                for part in parts
            )
            found = found[0:8] + found[8:16] + found[16:24]
            for head in range(HEADS):
                table_ref[head, pl.ds(8 + step * 8 + at, 1), 0:COLS] = found[head : head + 1]
        return carry

    lax.fori_loop(0, ROWS // 8, norm_step, 0, unroll=4)

    lane = lax.broadcasted_iota(jnp.int32, (BAND_ROWS, LANES), 1)
    row_base = place_ref[0]
    col_base = place_ref[1]

    def band_step(target, carry):
        first = first_ref[target]
        start = first - row_base + 8
        total = jnp.zeros((BAND_ROWS, LANES), F32)
        shift = col_base - (first - NEAR)
        for head in range(HEADS):
            rows = table_ref[head, pl.ds(start, BAND_ROWS), :]
            moved = pltpu.roll(rows, lax.rem(shift + head * BAND_COLS + 16 * LANES, LANES), 1)
            col = lane - head * BAND_COLS - shift
            keep = (lane // BAND_COLS == head) & (col >= 0) & (col < COLS)
            total = total + jnp.where(keep, moved, 0.0)
        band_ref[target] = total
        return carry

    lax.fori_loop(0, 16, band_step, 0, unroll=4)


def side(first, place, pair, pair_gain, gate_weight, bias_wide):
    whole = pl.BlockSpec(memory_space=pltpu.VMEM)
    scalars = pl.BlockSpec(memory_space=pltpu.SMEM)
    return pl.pallas_call(
        side_kernel,
        out_shape=(
            jax.ShapeDtypeStruct((ROWS, COLS, CHANNELS), F32),
            jax.ShapeDtypeStruct((16, BAND_ROWS, LANES), F32),
        ),
        in_specs=[scalars, scalars, whole, whole, whole, whole],
        out_specs=(whole, whole),
        scratch_shapes=[pltpu.VMEM((HEADS, ROWS + 32, LANES), F32)],
        compiler_params=pltpu.CompilerParams(vmem_limit_bytes=VMEM_LIMIT),
        cost_estimate=pl.CostEstimate(
            flops=8 * ROWS * COLS * 128 * 128, bytes_accessed=5000000, transcendentals=600000
        ),
        name="side",
    )(first, place, pair, pair_gain, gate_weight, bias_wide)


def atoms_kernel(
    base_ref,
    atoms_ref,
    before_ref,
    after_ref,
    band_ref,
    lane_start_ref,
    lane_end_ref,
    sub_start_ref,
    sub_end_ref,
    gain_ref,
    project_ref,
    output_ref,
    trans_gain_ref,
    up_ref,
    down_ref,
    out_ref,
):
    base = base_ref[0]
    own = atoms_ref[...].astype(F32)
    around = jnp.concatenate(
        [before_ref[...].astype(F32), own, after_ref[...].astype(F32)], 0
    )
    inputs = (layer_norm(around) * gain_ref[...]).astype(BF16)
    projected = jnp.dot(inputs, project_ref[...], preferred_element_type=F32)
    query = projected[HALO : HALO + ATOM_ROWS, 0:128].astype(BF16)
    key = projected[:, 128:256].astype(BF16)
    value = projected[:, 256:384].astype(BF16)
    gate = projected[HALO : HALO + ATOM_ROWS, 384:512].astype(BF16).astype(F32)

    query_atom = base + lax.broadcasted_iota(jnp.int32, (ATOM_ROWS, LANES), 0)
    query_hot = (
        ((query_atom >= lane_start_ref[...]) & (query_atom < lane_end_ref[...]))
        .astype(F32)
        .astype(BF16)
    )
    key_atom = base - HALO + lax.broadcasted_iota(jnp.int32, (LANES, KEY_ROWS), 1)
    key_hot = (
        ((key_atom >= sub_start_ref[...]) & (key_atom < sub_end_ref[...])).astype(F32)
    )
    token_head = lax.broadcasted_iota(jnp.int32, (LANES, KEY_ROWS), 0) // BAND_COLS

    band = jnp.sum(band_ref[...], 0)
    band = jnp.concatenate([band, jnp.zeros((LANES - BAND_ROWS, LANES), F32)], 0)
    picked = [
        jnp.dot(query_hot, part, preferred_element_type=F32).astype(BF16) for part in split3(band)
    ]

    window = lax.broadcasted_iota(jnp.int32, (ATOM_ROWS, KEY_ROWS), 0) // QUERIES
    place = lax.broadcasted_iota(jnp.int32, (ATOM_ROWS, KEY_ROWS), 1)
    near = place - window * QUERIES
    atom = base - HALO + place
    allowed = (near >= 0) & (near < KEYS) & (atom >= 0) & (atom < TOKENS * 32)
    lane_head = lax.broadcasted_iota(jnp.int32, (ATOM_ROWS, LANES), 1) // HEAD_DIM
    mixed = jnp.zeros((ATOM_ROWS, LANES), F32)
    for head in range(HEADS):
        own_query = jnp.where(lane_head == head, query.astype(F32), 0.0).astype(BF16)
        scores = lax.dot_general(
            own_query, key, (((1,), (1,)), ((), ())), preferred_element_type=F32
        ) * (HEAD_DIM**-0.5)
        head_hot = jnp.where(token_head == head, key_hot, 0.0).astype(BF16)
        for part in picked:
            scores = scores + jnp.dot(part, head_hot, preferred_element_type=F32)
        scores = jnp.where(allowed, scores, -jnp.inf)
        grown = jnp.exp(scores - jnp.max(scores, -1, keepdims=True))
        weights = (grown / jnp.sum(grown, -1, keepdims=True)).astype(BF16)
        mixed = mixed + jnp.where(
            lane_head == head, jnp.dot(weights, value, preferred_element_type=F32), 0.0
        )
    attended = (mixed * sigmoid(gate)).astype(BF16)
    state = own + jnp.dot(attended, output_ref[...], preferred_element_type=F32)
    inner = (layer_norm(state) * trans_gain_ref[...]).astype(BF16)
    upward = jnp.dot(inner, up_ref[...], preferred_element_type=F32)
    first, second = upward[:, :256], upward[:, 256:]
    hidden = (first * sigmoid(first) * second).astype(BF16)
    out_ref[...] = (
        state + jnp.dot(hidden, down_ref[...], preferred_element_type=F32)
    ).astype(BF16)


def atoms_block(base, *arrays):
    whole = pl.BlockSpec(memory_space=pltpu.VMEM)
    return pl.pallas_call(
        atoms_kernel,
        out_shape=jax.ShapeDtypeStruct((ATOM_ROWS, LANES), BF16),
        in_specs=[pl.BlockSpec(memory_space=pltpu.SMEM)] + [whole] * len(arrays),
        out_specs=whole,
        compiler_params=pltpu.CompilerParams(vmem_limit_bytes=VMEM_LIMIT),
        cost_estimate=pl.CostEstimate(
            flops=2 * 400 * 1000 * 1000, bytes_accessed=2000000, transcendentals=400000
        ),
        name="atoms_block",
    )(base, *arrays)


def on_device(
    pair,
    atoms,
    token_atoms,
    pair_gain,
    tri_proj,
    tri_out,
    out_gain,
    bias_weight,
    atom_gain,
    atom_proj,
    atom_out,
    trans_gain,
    trans_up,
    trans_down,
):
    row_id = lax.axis_index("row")
    col_id = lax.axis_index("col")
    device = row_id * 16 + col_id

    chunks, later_gain = edges(pair, pair_gain[None], tri_proj)
    arrived = lax.all_to_all(chunks, BOTH, 0, 0, tiled=True)

    ends = jnp.cumsum(token_atoms)
    starts = ends - token_atoms
    firsts_at = (row_id * 16 + jnp.arange(16, dtype=jnp.int32)) * ATOM_ROWS
    firsts = jnp.sum((ends[None, :] <= firsts_at[:, None]).astype(jnp.int32), 1)
    first = jnp.sum((ends <= device * ATOM_ROWS).astype(jnp.int32))
    far = jnp.full((LANES,), -1, jnp.int32)
    all_starts = jnp.concatenate([far, starts, far])
    all_ends = jnp.concatenate([far, ends, far])
    lane_start = lax.dynamic_slice(all_starts, (first + LANES,), (LANES,))
    lane_end = lax.dynamic_slice(all_ends, (first + LANES,), (LANES,))
    sub_start = lax.dynamic_slice(all_starts, (first + LANES - NEAR,), (BAND_COLS,))
    sub_end = lax.dynamic_slice(all_ends, (first + LANES - NEAR,), (BAND_COLS,))

    bias_wide = jnp.pad(bias_weight.T, ((0, 4), (0, 0)))
    place = jnp.stack([row_id * ROWS, col_id * COLS]).astype(jnp.int32)
    gate, bands = side(firsts, place, pair, later_gain, tri_proj, bias_wide)
    band = lax.all_to_all(bands, "col", 0, 0, tiled=True)

    ring = list(range(127))
    before = lax.ppermute(atoms[ATOM_ROWS - HALO :], BOTH, [(at, at + 1) for at in ring])
    after = lax.ppermute(atoms[:HALO], BOTH, [(at + 1, at) for at in ring])
    atoms_out = atoms_block(
        (device * ATOM_ROWS).astype(jnp.int32)[None],
        atoms,
        before,
        after,
        band,
        lane_start[None],
        lane_end[None],
        jnp.tile(sub_start, HEADS)[:, None],
        jnp.tile(sub_end, HEADS)[:, None],
        atom_gain[None],
        atom_proj,
        atom_out,
        trans_gain[None],
        trans_up,
        trans_down,
    )

    sums = triangle(arrived)
    returned = lax.all_to_all(sums, BOTH, 0, 0, tiled=True)
    pair_out = update_pair(returned, pair, gate, out_gain[None], tri_out)
    return (pair_out, atoms_out)


def solution(mesh):
    return jax.shard_map(
        on_device,
        mesh=mesh,
        in_specs=(P("row", "col", None), P(BOTH, None)) + (P(),) * 12,
        out_specs=(P("row", "col", None), P(BOTH, None)),
        check_vma=False,
    )
```

```python
import functools

import jax
import jax.numpy as jnp
from jax import lax
from jax.experimental import pallas as pl
from jax.experimental.pallas import tpu as pltpu
from jax.sharding import PartitionSpec as P

ROWS = 96
COLS = 48
LANES = 128
CHANNELS = 128
TOKENS = 768
QUERIES = 32
KEYS = 128
HALO = 48
ATOM_ROWS = 192
KEY_ROWS = ATOM_ROWS + 2 * HALO
HEADS = 4
HEAD_DIM = 32
NEAR = 5
BAND_ROWS = 16
BAND_COLS = 32
EDGE_ROWS = 72
SUM_ROWS = 40
EPSILON = 1e-05
BOTH = ("row", "col")
VMEM_LIMIT = 20 * 1024 * 1024

F32 = jnp.float32
BF16 = jnp.bfloat16


def layer_norm(values):
    center = values - jnp.mean(values, -1, keepdims=True)
    return center * lax.rsqrt(jnp.mean(center * center, -1, keepdims=True) + EPSILON)


def sigmoid(values):
    return 0.5 * jnp.tanh(0.5 * values) + 0.5


def edges_kernel(
    pair_ref,
    gain_ref,
    weight_ref,
    edges_ref,
    gain_out_ref,
    tile_ref,
    gain_in_ref,
    weight_in_ref,
    wide_ref,
    stage_ref,
    ready_ref,
    in_sems,
    param_sems,
    out_sems,
):
    steps = ROWS // 8
    gain_copy = pltpu.make_async_copy(gain_ref, gain_in_ref, param_sems.at[0])
    weight_copy = pltpu.make_async_copy(weight_ref, weight_in_ref, param_sems.at[1])
    tile_copies = [
        pltpu.make_async_copy(
            pair_ref.at[pl.ds(step * 8, 8)], tile_ref.at[pl.ds(step * 8, 8)], in_sems.at[step]
        )
        for step in range(steps)
    ]
    gain_copy.start()
    for copy in tile_copies:
        copy.start()
    weight_copy.start()
    gain_copy.wait()
    gain_out_ref[...] = gain_in_ref[...]
    gain = jnp.broadcast_to(gain_in_ref[...], (2 * LANES, CHANNELS)).T
    eye = (
        lax.broadcasted_iota(jnp.int32, (CHANNELS, CHANNELS), 0)
        == lax.broadcasted_iota(jnp.int32, (CHANNELS, CHANNELS), 1)
    ).astype(F32).astype(BF16)

    def norm_step(step, carry):
        rows = pl.ds(step * 8, 8)
        pltpu.make_async_copy(pair_ref.at[rows], tile_ref.at[rows], in_sems.at[step]).wait()
        tile = tile_ref[rows].astype(F32).reshape(8 * COLS, CHANNELS)
        wide_ref[pl.ds(pl.multiple_of(step * 8 * COLS, 8 * COLS), 8 * COLS), :] = tile
        return carry

    lax.fori_loop(0, steps, norm_step, 0, unroll=3)
    weight_copy.wait()
    weight = weight_in_ref[:, :512].T

    def packed(col, third, extra):
        main = wide_ref[pl.ds(col, ROWS, stride=COLS), :]
        rest = wide_ref[pl.ds(third * 32 * COLS + extra, 32, stride=COLS), :]
        return jnp.concatenate([main, rest], 0).astype(BF16)

    def emit(sources, count):
        for at in range(0, count, 2):
            rows = jnp.concatenate([packed(*source) for source in sources[at : at + 2]], 0)
            flipped = lax.dot_general(
                eye, rows, (((1,), (1,)), ((), ())), preferred_element_type=F32
            )
            center = flipped - jnp.mean(flipped, 0, keepdims=True)
            scale = lax.rsqrt(jnp.mean(center * center, 0, keepdims=True) + EPSILON)
            inputs = (center * scale * gain).astype(BF16)
            project = jnp.dot(weight, inputs, preferred_element_type=F32)
            left = sigmoid(project[:128]) * project[128:256]
            right = sigmoid(project[256:384]) * project[384:]
            for half in range(2):
                lanes = slice(half * LANES, (half + 1) * LANES)
                stage_ref[pl.ds(at + half, CHANNELS, stride=24), :] = left[:, lanes]
                stage_ref[pl.ds(count + at + half, CHANNELS, stride=24), :] = right[:, lanes]

    def block_copy(group):
        rows = pl.ds(pl.multiple_of(group * 16, 16), 16)
        return pltpu.make_async_copy(
            ready_ref.at[group], edges_ref.at[:, rows, :], out_sems.at[group]
        )

    def block(group, carry):
        sources = []
        for at in range(8):
            third = jnp.where(group < 3, group, at // 4)
            extra = jnp.where(group < 3, 36 + at, 44 + at % 4)
            sources.append((group * 8 + at, third, extra))
        emit(sources, 8)
        ready_ref[group] = stage_ref[...].reshape(CHANNELS, 24, LANES)[:, :16].astype(BF16)
        block_copy(group).start()
        return carry

    lax.fori_loop(0, 4, block, 0, unroll=4)
    emit([(32 + at, 2, 44 + at) for at in range(4)], 4)
    ready_ref[4, :, 0:8, :] = stage_ref[...].reshape(CHANNELS, 24, LANES)[:, :8].astype(BF16)
    last = pltpu.make_async_copy(
        ready_ref.at[4, :, pl.ds(0, 8), :], edges_ref.at[:, pl.ds(64, 8), :], out_sems.at[4]
    )
    last.start()
    for group in range(4):
        block_copy(group).wait()
    last.wait()


def edges(pair, pair_gain, weight):
    far = pl.BlockSpec(memory_space=pltpu.HBM)
    return pl.pallas_call(
        edges_kernel,
        out_shape=(
            jax.ShapeDtypeStruct((CHANNELS, EDGE_ROWS, LANES), BF16),
            jax.ShapeDtypeStruct((1, CHANNELS), F32),
        ),
        in_specs=[far] * 3,
        out_specs=(far, pl.BlockSpec(memory_space=pltpu.VMEM)),
        scratch_shapes=[
            pltpu.VMEM((ROWS, COLS, CHANNELS), BF16),
            pltpu.VMEM((1, CHANNELS), F32),
            pltpu.VMEM((CHANNELS, 640), BF16),
            pltpu.VMEM((ROWS * COLS, CHANNELS), F32),
            pltpu.VMEM((CHANNELS * 24, LANES), F32),
            pltpu.VMEM((5, CHANNELS, 16, LANES), BF16),
            pltpu.SemaphoreType.DMA((ROWS // 8,)),
            pltpu.SemaphoreType.DMA((2,)),
            pltpu.SemaphoreType.DMA((5,)),
        ],
        compiler_params=pltpu.CompilerParams(vmem_limit_bytes=56 * 1024 * 1024),
        cost_estimate=pl.CostEstimate(
            flops=2 * ROWS * COLS * 128 * 512, bytes_accessed=4000000, transcendentals=1200000
        ),
        name="edges",
    )(pair, pair_gain, weight)


def triangle_kernel(
    arrived_ref,
    sums_ref,
    chunks_ref,
    left_ref,
    right_ref,
    flip_ref,
    out_ref,
    ready_ref,
    in_sems,
    sems,
):
    def row_load(row):
        part = pl.ds(pl.multiple_of(row * 16, 16), 16)
        return pltpu.make_async_copy(arrived_ref.at[part], chunks_ref.at[part], in_sems.at[row])

    for row in range(8):
        row_load(row).start()

    lane = lax.broadcasted_iota(jnp.int32, (8, LANES), 1)
    low = lax.broadcasted_iota(jnp.int32, (8, LANES), 0) < 4

    def thirds(first, second, third):
        return jnp.where(
            lane < 32,
            pltpu.roll(first, 32, 1),
            jnp.where(lane < 64, pltpu.roll(second, 64, 1), pltpu.roll(third, 96, 1)),
        )

    def gather_row(row, carry):
        row_load(row).wait()
        lanes = pl.ds(pl.multiple_of(row * LANES, LANES), LANES)

        def gather(col, carry):
            chunk = chunks_ref[row * 16 + col].astype(F32)
            part = [chunk[at * 8 : at * 8 + 8] for at in range(9)]
            tail = part[8]
            turned = pltpu.roll(tail, 4, 0)
            at_rows = pl.ds(pl.multiple_of(col * COLS, COLS), COLS)
            left, right = part[0:8:2], part[1:8:2]
            for ref, main, last, spare in (
                (left_ref, left, tail, turned),
                (right_ref, right, turned, tail),
            ):
                fine = thirds(pltpu.roll(main[3], 4, 0), main[3], spare)
                whole = jnp.concatenate(
                    main + [thirds(main[0], main[1], main[2]), jnp.where(low, last, fine)], 0
                )
                ref[at_rows, lanes] = whole.astype(BF16)
            return carry

        lax.fori_loop(0, 16, gather, 0, unroll=16)
        flip_ref[lanes, :] = right_ref[:, lanes].T
        return carry

    lax.fori_loop(0, 8, gather_row, 0, unroll=True)

    def row_copy(row):
        part = pl.ds(pl.multiple_of(row * 16, 16), 16)
        return pltpu.make_async_copy(ready_ref.at[part], sums_ref.at[part], sems.at[row])

    def product(pair_at, carry):
        lanes = pl.ds(pl.multiple_of(pair_at * 256, 256), 256)
        out_ref[...] = jnp.dot(
            flip_ref[...], left_ref[:, lanes], preferred_element_type=F32
        )
        for half in range(2):
            row = pair_at * 2 + half

            def pack(col_pair, carry):
                for side in range(2):
                    start = pl.multiple_of(col_pair * LANES + side * COLS, 16)
                    block = out_ref[pl.ds(start, COLS), half * LANES : (half + 1) * LANES]
                    rest = block[40:48]
                    head = [
                        jnp.where(
                            lane < 96, block[at * 8 : at * 8 + 8], pltpu.roll(rest, 96 - 32 * at, 1)
                        )
                        for at in range(3)
                    ]
                    whole = jnp.concatenate(head + [block[24:40]], 0)
                    ready_ref[row * 16 + col_pair * 2 + side] = whole.astype(BF16)
                return carry

            lax.fori_loop(0, 8, pack, 0, unroll=8)
            row_copy(row).start()
        return carry

    lax.fori_loop(0, 4, product, 0, unroll=True)
    for row in range(8):
        row_copy(row).wait()


def triangle(chunks):
    return pl.pallas_call(
        triangle_kernel,
        out_shape=jax.ShapeDtypeStruct((CHANNELS, SUM_ROWS, LANES), BF16),
        in_specs=[pl.BlockSpec(memory_space=pltpu.HBM)],
        out_specs=pl.BlockSpec(memory_space=pltpu.HBM),
        scratch_shapes=[
            pltpu.VMEM((CHANNELS, EDGE_ROWS, LANES), BF16),
            pltpu.VMEM((TOKENS, 1024), BF16),
            pltpu.VMEM((TOKENS, 1024), BF16),
            pltpu.VMEM((1024, TOKENS), BF16),
            pltpu.VMEM((1024, 256), F32),
            pltpu.VMEM((CHANNELS, SUM_ROWS, LANES), BF16),
            pltpu.SemaphoreType.DMA((8,)),
            pltpu.SemaphoreType.DMA((8,)),
        ],
        compiler_params=pltpu.CompilerParams(vmem_limit_bytes=52 * 1024 * 1024),
        cost_estimate=pl.CostEstimate(
            flops=2 * 1024 * 1024 * 768, bytes_accessed=4000000, transcendentals=0
        ),
        name="triangle",
    )(chunks)


def update_kernel(
    sums_ref,
    pair_ref,
    gate_ref,
    gain_ref,
    weight_ref,
    out_ref,
    pair_in_ref,
    gate_in_ref,
    ready_ref,
    normed_ref,
    update_ref,
    pair_sems,
    gate_sems,
    out_sems,
):
    parts = [pl.ds(at * 24, 24) for at in range(4)]
    loads = []
    for at, part in enumerate(parts):
        loads.append(
            (
                pltpu.make_async_copy(pair_ref.at[part], pair_in_ref.at[part], pair_sems.at[at]),
                pltpu.make_async_copy(gate_ref.at[part], gate_in_ref.at[part], gate_sems.at[at]),
            )
        )
        for copy in loads[-1]:
            copy.start()
    gain = jnp.broadcast_to(gain_ref[...], (CHANNELS, LANES)).T
    weight = weight_ref[...]

    for step in range(SUM_ROWS // 8):
        tile = sums_ref[:, step * 8 : step * 8 + 8, :].astype(F32)
        center = tile - jnp.mean(tile, 0, keepdims=True)
        scale = lax.rsqrt(jnp.mean(center * center, 0, keepdims=True) + EPSILON)
        normed_ref[...] = (center * scale).reshape(CHANNELS * 8, LANES)
        for at in range(8):
            block = (normed_ref[pl.ds(at, CHANNELS, stride=8), :] * gain).astype(BF16)
            update = lax.dot_general(
                block, weight, (((0,), (0,)), ((), ())), preferred_element_type=F32
            )
            update_ref[pl.ds(step * 8 + at, ROWS, stride=COLS), :] = update[:ROWS]
            if step < 3:
                start = step * 32 * COLS + 40 + at
                update_ref[pl.ds(start, 32, stride=COLS), :] = update[ROWS:]

    stores = []
    for at, part in enumerate(parts):
        for copy in loads[at]:
            copy.wait()
        for step in range(at * 3, at * 3 + 3):
            rows = pl.ds(step * 8, 8)
            update = update_ref[pl.ds(step * 8 * COLS, 8 * COLS), :].reshape(8, COLS, CHANNELS)
            ready_ref[rows] = (
                pair_in_ref[rows].astype(F32) + gate_in_ref[rows] * update
            ).astype(BF16)
        copy = pltpu.make_async_copy(ready_ref.at[part], out_ref.at[part], out_sems.at[at])
        copy.start()
        stores.append(copy)
    for copy in stores:
        copy.wait()


def update_pair(sums, pair, gate, out_gain, tri_out):
    far = pl.BlockSpec(memory_space=pltpu.HBM)
    near = pl.BlockSpec(memory_space=pltpu.VMEM)
    return pl.pallas_call(
        update_kernel,
        out_shape=jax.ShapeDtypeStruct((ROWS, COLS, CHANNELS), BF16),
        in_specs=[near, far, far, near, near],
        out_specs=far,
        scratch_shapes=[
            pltpu.VMEM((ROWS, COLS, CHANNELS), BF16),
            pltpu.VMEM((ROWS, COLS, CHANNELS), F32),
            pltpu.VMEM((ROWS, COLS, CHANNELS), BF16),
            pltpu.VMEM((CHANNELS * 8, LANES), F32),
            pltpu.VMEM((ROWS * COLS, CHANNELS), F32),
            pltpu.SemaphoreType.DMA((4,)),
            pltpu.SemaphoreType.DMA((4,)),
            pltpu.SemaphoreType.DMA((4,)),
        ],
        compiler_params=pltpu.CompilerParams(vmem_limit_bytes=50 * 1024 * 1024),
        cost_estimate=pl.CostEstimate(
            flops=2 * ROWS * COLS * 128 * 128, bytes_accessed=6000000, transcendentals=5000
        ),
        name="update_pair",
    )(sums, pair, gate, out_gain, tri_out)


def split3(values):
    high = values.astype(BF16)
    rest = values - high.astype(F32)
    middle = rest.astype(BF16)
    low = (rest - middle.astype(F32)).astype(BF16)
    return high, middle, low


def side_kernel(
    first_ref, place_ref, pair_ref, gain_ref, weight_ref, bias_ref, gate_ref, band_ref, table_ref
):
    gain = gain_ref[...]
    weight = weight_ref[:, 512:]
    bias = jnp.concatenate([part.astype(F32) for part in split3(bias_ref[...])], 0).astype(BF16)
    table_ref[...] = jnp.zeros_like(table_ref)

    def norm_step(step, carry):
        tile = pair_ref[pl.ds(step * 8, 8)].astype(F32).reshape(8 * COLS, CHANNELS)
        normed = layer_norm(tile)
        inputs = (normed * gain).astype(BF16)
        gate = sigmoid(jnp.dot(inputs, weight, preferred_element_type=F32))
        gate_ref[pl.ds(step * 8, 8)] = gate.reshape(8, COLS, CHANNELS)
        parts = split3(normed)
        for at in range(8):
            rows = slice(at * COLS, (at + 1) * COLS)
            found = sum(
                lax.dot_general(
                    bias, part[rows], (((1,), (1,)), ((), ())), preferred_element_type=F32
                )
                for part in parts
            )
            found = found[0:8] + found[8:16] + found[16:24]
            for head in range(HEADS):
                table_ref[head, pl.ds(8 + step * 8 + at, 1), 0:COLS] = found[head : head + 1]
        return carry

    lax.fori_loop(0, ROWS // 8, norm_step, 0, unroll=4)

    lane = lax.broadcasted_iota(jnp.int32, (BAND_ROWS, LANES), 1)
    row_base = place_ref[0]
    col_base = place_ref[1]

    def band_step(slot, carry):
        first = first_ref[jnp.bitwise_xor(slot, place_ref[2])]
        start = first - row_base + 8
        total = jnp.zeros((BAND_ROWS, LANES), F32)
        shift = col_base - (first - NEAR)
        for head in range(HEADS):
            rows = table_ref[head, pl.ds(start, BAND_ROWS), :]
            moved = pltpu.roll(rows, lax.rem(shift + head * BAND_COLS + 16 * LANES, LANES), 1)
            col = lane - head * BAND_COLS - shift
            keep = (lane // BAND_COLS == head) & (col >= 0) & (col < COLS)
            total = total + jnp.where(keep, moved, 0.0)
        band_ref[slot] = total
        return carry

    lax.fori_loop(0, 16, band_step, 0, unroll=4)


def side(first, place, pair, pair_gain, gate_weight, bias_wide):
    whole = pl.BlockSpec(memory_space=pltpu.VMEM)
    scalars = pl.BlockSpec(memory_space=pltpu.SMEM)
    return pl.pallas_call(
        side_kernel,
        out_shape=(
            jax.ShapeDtypeStruct((ROWS, COLS, CHANNELS), F32),
            jax.ShapeDtypeStruct((16, BAND_ROWS, LANES), F32),
        ),
        in_specs=[scalars, scalars, whole, whole, whole, whole],
        out_specs=(whole, whole),
        scratch_shapes=[pltpu.VMEM((HEADS, ROWS + 32, LANES), F32)],
        compiler_params=pltpu.CompilerParams(vmem_limit_bytes=VMEM_LIMIT),
        cost_estimate=pl.CostEstimate(
            flops=8 * ROWS * COLS * 128 * 128, bytes_accessed=5000000, transcendentals=600000
        ),
        name="side",
    )(first, place, pair, pair_gain, gate_weight, bias_wide)


def atoms_kernel(
    base_ref,
    atoms_ref,
    before_ref,
    after_ref,
    band0_ref,
    band1_ref,
    band2_ref,
    band3_ref,
    lane_start_ref,
    lane_end_ref,
    sub_start_ref,
    sub_end_ref,
    gain_ref,
    project_ref,
    output_ref,
    trans_gain_ref,
    up_ref,
    down_ref,
    out_ref,
):
    base = base_ref[0]
    own = atoms_ref[...].astype(F32)
    around = jnp.concatenate(
        [before_ref[...].astype(F32), own, after_ref[...].astype(F32)], 0
    )
    inputs = (layer_norm(around) * gain_ref[...]).astype(BF16)
    projected = jnp.dot(inputs, project_ref[...], preferred_element_type=F32)
    query = projected[HALO : HALO + ATOM_ROWS, 0:128].astype(BF16)
    key = projected[:, 128:256].astype(BF16)
    value = projected[:, 256:384].astype(BF16)
    gate = projected[HALO : HALO + ATOM_ROWS, 384:512].astype(BF16).astype(F32)

    query_atom = base + lax.broadcasted_iota(jnp.int32, (ATOM_ROWS, LANES), 0)
    query_hot = (
        ((query_atom >= lane_start_ref[...]) & (query_atom < lane_end_ref[...]))
        .astype(F32)
        .astype(BF16)
    )
    key_atom = base - HALO + lax.broadcasted_iota(jnp.int32, (LANES, KEY_ROWS), 1)
    key_hot = (
        ((key_atom >= sub_start_ref[...]) & (key_atom < sub_end_ref[...])).astype(F32)
    )
    token_head = lax.broadcasted_iota(jnp.int32, (LANES, KEY_ROWS), 0) // BAND_COLS

    band = band0_ref[0] + band1_ref[0] + band2_ref[0] + band3_ref[0]
    band = jnp.concatenate([band, jnp.zeros((LANES - BAND_ROWS, LANES), F32)], 0)
    picked = [
        jnp.dot(query_hot, part, preferred_element_type=F32).astype(BF16) for part in split3(band)
    ]

    window = lax.broadcasted_iota(jnp.int32, (ATOM_ROWS, KEY_ROWS), 0) // QUERIES
    place = lax.broadcasted_iota(jnp.int32, (ATOM_ROWS, KEY_ROWS), 1)
    near = place - window * QUERIES
    atom = base - HALO + place
    allowed = (near >= 0) & (near < KEYS) & (atom >= 0) & (atom < TOKENS * 32)
    lane_head = lax.broadcasted_iota(jnp.int32, (ATOM_ROWS, LANES), 1) // HEAD_DIM
    mixed = jnp.zeros((ATOM_ROWS, LANES), F32)
    for head in range(HEADS):
        own_query = jnp.where(lane_head == head, query.astype(F32), 0.0).astype(BF16)
        scores = lax.dot_general(
            own_query, key, (((1,), (1,)), ((), ())), preferred_element_type=F32
        ) * (HEAD_DIM**-0.5)
        head_hot = jnp.where(token_head == head, key_hot, 0.0).astype(BF16)
        for part in picked:
            scores = scores + jnp.dot(part, head_hot, preferred_element_type=F32)
        scores = jnp.where(allowed, scores, -jnp.inf)
        grown = jnp.exp(scores - jnp.max(scores, -1, keepdims=True))
        weights = (grown / jnp.sum(grown, -1, keepdims=True)).astype(BF16)
        mixed = mixed + jnp.where(
            lane_head == head, jnp.dot(weights, value, preferred_element_type=F32), 0.0
        )
    attended = (mixed * sigmoid(gate)).astype(BF16)
    state = own + jnp.dot(attended, output_ref[...], preferred_element_type=F32)
    inner = (layer_norm(state) * trans_gain_ref[...]).astype(BF16)
    upward = jnp.dot(inner, up_ref[...], preferred_element_type=F32)
    first, second = upward[:, :256], upward[:, 256:]
    hidden = (first * sigmoid(first) * second).astype(BF16)
    out_ref[...] = (
        state + jnp.dot(hidden, down_ref[...], preferred_element_type=F32)
    ).astype(BF16)


def atoms_block(base, *arrays):
    whole = pl.BlockSpec(memory_space=pltpu.VMEM)
    return pl.pallas_call(
        atoms_kernel,
        out_shape=jax.ShapeDtypeStruct((ATOM_ROWS, LANES), BF16),
        in_specs=[pl.BlockSpec(memory_space=pltpu.SMEM)] + [whole] * len(arrays),
        out_specs=whole,
        compiler_params=pltpu.CompilerParams(vmem_limit_bytes=VMEM_LIMIT),
        cost_estimate=pl.CostEstimate(
            flops=2 * 400 * 1000 * 1000, bytes_accessed=2000000, transcendentals=400000
        ),
        name="atoms_block",
    )(base, *arrays)


def on_device(
    pair,
    atoms,
    token_atoms,
    pair_gain,
    tri_proj,
    tri_out,
    out_gain,
    bias_weight,
    atom_gain,
    atom_proj,
    atom_out,
    trans_gain,
    trans_up,
    trans_down,
):
    row_id = lax.axis_index("row")
    col_id = lax.axis_index("col")
    device = row_id * 16 + col_id

    chunks, later_gain = edges(pair, pair_gain[None], tri_proj)
    arrived = lax.all_to_all(chunks, BOTH, 0, 0, tiled=True)

    ends = jnp.cumsum(token_atoms)
    starts = ends - token_atoms
    firsts_at = (row_id * 16 + jnp.arange(16, dtype=jnp.int32)) * ATOM_ROWS
    firsts = jnp.sum((ends[None, :] <= firsts_at[:, None]).astype(jnp.int32), 1)
    first = jnp.sum((ends <= device * ATOM_ROWS).astype(jnp.int32))
    far = jnp.full((LANES,), -1, jnp.int32)
    all_starts = jnp.concatenate([far, starts, far])
    all_ends = jnp.concatenate([far, ends, far])
    lane_start = lax.dynamic_slice(all_starts, (first + LANES,), (LANES,))
    lane_end = lax.dynamic_slice(all_ends, (first + LANES,), (LANES,))
    sub_start = lax.dynamic_slice(all_starts, (first + LANES - NEAR,), (BAND_COLS,))
    sub_end = lax.dynamic_slice(all_ends, (first + LANES - NEAR,), (BAND_COLS,))

    bias_wide = jnp.pad(bias_weight.T, ((0, 4), (0, 0)))
    place = jnp.stack([row_id * ROWS, col_id * COLS, col_id]).astype(jnp.int32)
    gate, bands = side(firsts, place, pair, later_gain, tri_proj, bias_wide)
    def exchange(values, size):
        parts = [values[:size]]
        for at in range(1, 4):
            pairs = [(device, device ^ (at * size)) for device in range(16)]
            parts.append(lax.ppermute(values[at * size : (at + 1) * size], "col", pairs))
        return parts

    halves = exchange(bands, 4)
    arrived, *halves = lax.optimization_barrier((arrived, *halves))
    parts = exchange(sum(halves), 1)
    ring = list(range(127))
    before = lax.ppermute(atoms[ATOM_ROWS - HALO :], BOTH, [(at, at + 1) for at in ring])
    after = lax.ppermute(atoms[:HALO], BOTH, [(at + 1, at) for at in ring])
    atoms_out = atoms_block(
        (device * ATOM_ROWS).astype(jnp.int32)[None],
        atoms,
        before,
        after,
        *parts,
        lane_start[None],
        lane_end[None],
        jnp.tile(sub_start, HEADS)[:, None],
        jnp.tile(sub_end, HEADS)[:, None],
        atom_gain[None],
        atom_proj,
        atom_out,
        trans_gain[None],
        trans_up,
        trans_down,
    )

    sums = triangle(arrived)
    returned = lax.all_to_all(sums, BOTH, 0, 0, tiled=True)
    pair_out = update_pair(returned, pair, gate, out_gain[None], tri_out)
    return (pair_out, atoms_out)


def solution(mesh):
    return jax.shard_map(
        on_device,
        mesh=mesh,
        in_specs=(P("row", "col", None), P(BOTH, None)) + (P(),) * 12,
        out_specs=(P("row", "col", None), P(BOTH, None)),
        check_vma=False,
    )
```

```python
import functools

import jax
import jax.numpy as jnp
from jax import lax
from jax.experimental import pallas as pl
from jax.experimental.pallas import tpu as pltpu
from jax.sharding import PartitionSpec as P

ROWS = 96
COLS = 48
LANES = 128
CHANNELS = 128
TOKENS = 768
QUERIES = 32
KEYS = 128
HALO = 48
ATOM_ROWS = 192
KEY_ROWS = ATOM_ROWS + 2 * HALO
HEADS = 4
HEAD_DIM = 32
NEAR = 5
BAND_ROWS = 16
BAND_COLS = 32
EDGE_ROWS = 72
WIDE = 56
SUM_ROWS = 40
EPSILON = 1e-05
BOTH = ("row", "col")
VMEM_LIMIT = 20 * 1024 * 1024

F32 = jnp.float32
BF16 = jnp.bfloat16


def layer_norm(values):
    center = values - jnp.mean(values, -1, keepdims=True)
    return center * lax.rsqrt(jnp.mean(center * center, -1, keepdims=True) + EPSILON)


def sigmoid(values):
    return 0.5 * jnp.tanh(0.5 * values) + 0.5


def edges_kernel(
    pair_ref,
    gain_ref,
    weight_ref,
    edges_ref,
    gain_out_ref,
    tile_ref,
    gain_in_ref,
    weight_in_ref,
    wide_ref,
    stage_ref,
    ready_ref,
    in_sems,
    param_sems,
    out_sems,
):
    steps = ROWS // 8
    gain_copy = pltpu.make_async_copy(gain_ref, gain_in_ref, param_sems.at[0])
    weight_copy = pltpu.make_async_copy(weight_ref, weight_in_ref, param_sems.at[1])
    tile_copies = [
        pltpu.make_async_copy(
            pair_ref.at[pl.ds(step * 8, 8)], tile_ref.at[pl.ds(step * 8, 8)], in_sems.at[step]
        )
        for step in range(steps)
    ]
    gain_copy.start()
    for copy in tile_copies:
        copy.start()
    weight_copy.start()
    gain_copy.wait()
    gain_out_ref[...] = gain_in_ref[...]
    gain = jnp.broadcast_to(gain_in_ref[...], (2 * LANES, CHANNELS)).T
    eye = (
        lax.broadcasted_iota(jnp.int32, (CHANNELS, CHANNELS), 0)
        == lax.broadcasted_iota(jnp.int32, (CHANNELS, CHANNELS), 1)
    ).astype(F32).astype(BF16)

    def norm_step(step, carry):
        rows = pl.ds(step * 8, 8)
        pltpu.make_async_copy(pair_ref.at[rows], tile_ref.at[rows], in_sems.at[step]).wait()
        tile = tile_ref[rows].astype(F32)
        for at in range(8):
            start = pl.multiple_of((step * 8 + at) * WIDE, 8)
            wide_ref[pl.ds(start, COLS), :] = tile[at]
        return carry

    lax.fori_loop(0, steps, norm_step, 0, unroll=3)
    weight_copy.wait()
    weight = weight_in_ref[:, :512].T

    def packed(col, third, extra):
        main = wide_ref[pl.ds(col, ROWS, stride=WIDE), :]
        rest = wide_ref[pl.ds(third * 32 * WIDE + extra, 32, stride=WIDE), :]
        return jnp.concatenate([main, rest], 0).astype(BF16)

    def emit(sources, count):
        for at in range(0, count, 2):
            rows = jnp.concatenate([packed(*source) for source in sources[at : at + 2]], 0)
            flipped = lax.dot_general(
                eye, rows, (((1,), (1,)), ((), ())), preferred_element_type=F32
            )
            center = flipped - jnp.mean(flipped, 0, keepdims=True)
            scale = lax.rsqrt(jnp.mean(center * center, 0, keepdims=True) + EPSILON)
            inputs = (center * scale * gain).astype(BF16)
            project = jnp.dot(weight, inputs, preferred_element_type=F32)
            left = sigmoid(project[:128]) * project[128:256]
            right = sigmoid(project[256:384]) * project[384:]
            for half in range(2):
                lanes = slice(half * LANES, (half + 1) * LANES)
                stage_ref[pl.ds(at + half, CHANNELS, stride=24), :] = left[:, lanes]
                stage_ref[pl.ds(count + at + half, CHANNELS, stride=24), :] = right[:, lanes]

    def block_copy(group):
        rows = pl.ds(pl.multiple_of(group * 16, 16), 16)
        return pltpu.make_async_copy(
            ready_ref.at[group], edges_ref.at[:, rows, :], out_sems.at[group]
        )

    def block(group, carry):
        sources = []
        for at in range(8):
            third = jnp.where(group < 3, group, at // 4)
            extra = jnp.where(group < 3, 36 + at, 44 + at % 4)
            sources.append((group * 8 + at, third, extra))
        emit(sources, 8)
        ready_ref[group] = stage_ref[...].reshape(CHANNELS, 24, LANES)[:, :16].astype(BF16)
        block_copy(group).start()
        return carry

    lax.fori_loop(0, 4, block, 0, unroll=4)
    emit([(32 + at, 2, 44 + at) for at in range(4)], 4)
    ready_ref[4, :, 0:8, :] = stage_ref[...].reshape(CHANNELS, 24, LANES)[:, :8].astype(BF16)
    last = pltpu.make_async_copy(
        ready_ref.at[4, :, pl.ds(0, 8), :], edges_ref.at[:, pl.ds(64, 8), :], out_sems.at[4]
    )
    last.start()
    for group in range(4):
        block_copy(group).wait()
    last.wait()


def edges(pair, pair_gain, weight):
    far = pl.BlockSpec(memory_space=pltpu.HBM)
    return pl.pallas_call(
        edges_kernel,
        out_shape=(
            jax.ShapeDtypeStruct((CHANNELS, EDGE_ROWS, LANES), BF16),
            jax.ShapeDtypeStruct((1, CHANNELS), F32),
        ),
        in_specs=[far] * 3,
        out_specs=(far, pl.BlockSpec(memory_space=pltpu.VMEM)),
        scratch_shapes=[
            pltpu.VMEM((ROWS, COLS, CHANNELS), BF16),
            pltpu.VMEM((1, CHANNELS), F32),
            pltpu.VMEM((CHANNELS, 640), BF16),
            pltpu.VMEM((ROWS * WIDE, CHANNELS), F32),
            pltpu.VMEM((CHANNELS * 24, LANES), F32),
            pltpu.VMEM((5, CHANNELS, 16, LANES), BF16),
            pltpu.SemaphoreType.DMA((ROWS // 8,)),
            pltpu.SemaphoreType.DMA((2,)),
            pltpu.SemaphoreType.DMA((5,)),
        ],
        compiler_params=pltpu.CompilerParams(vmem_limit_bytes=56 * 1024 * 1024),
        cost_estimate=pl.CostEstimate(
            flops=2 * ROWS * COLS * 128 * 512, bytes_accessed=4000000, transcendentals=1200000
        ),
        name="edges",
    )(pair, pair_gain, weight)


def triangle_kernel(
    arrived_ref,
    sums_ref,
    chunks_ref,
    left_ref,
    right_ref,
    flip_ref,
    out_ref,
    ready_ref,
    in_sems,
    sems,
):
    def row_load(row):
        part = pl.ds(pl.multiple_of(row * 16, 16), 16)
        return pltpu.make_async_copy(arrived_ref.at[part], chunks_ref.at[part], in_sems.at[row])

    for row in range(8):
        row_load(row).start()

    lane = lax.broadcasted_iota(jnp.int32, (8, LANES), 1)
    low = lax.broadcasted_iota(jnp.int32, (8, LANES), 0) < 4

    def thirds(first, second, third):
        return jnp.where(
            lane < 32,
            pltpu.roll(first, 32, 1),
            jnp.where(lane < 64, pltpu.roll(second, 64, 1), pltpu.roll(third, 96, 1)),
        )

    def gather_row(row, carry):
        row_load(row).wait()
        lanes = pl.ds(pl.multiple_of(row * LANES, LANES), LANES)

        def gather(col, carry):
            chunk = chunks_ref[row * 16 + col].astype(F32)
            part = [chunk[at * 8 : at * 8 + 8] for at in range(9)]
            tail = part[8]
            turned = pltpu.roll(tail, 4, 0)
            at_rows = pl.ds(pl.multiple_of(col * COLS, COLS), COLS)
            left, right = part[0:8:2], part[1:8:2]
            for ref, main, last, spare in (
                (left_ref, left, tail, turned),
                (right_ref, right, turned, tail),
            ):
                fine = thirds(pltpu.roll(main[3], 4, 0), main[3], spare)
                whole = jnp.concatenate(
                    main + [thirds(main[0], main[1], main[2]), jnp.where(low, last, fine)], 0
                )
                ref[at_rows, lanes] = whole.astype(BF16)
            return carry

        lax.fori_loop(0, 16, gather, 0, unroll=16)
        flip_ref[pl.ds(pl.multiple_of(row * ROWS, ROWS), ROWS), :] = right_ref[:, lanes].T[:ROWS]
        return carry

    lax.fori_loop(0, 8, gather_row, 0, unroll=True)

    def row_copy(row):
        part = pl.ds(pl.multiple_of(row * 16, 16), 16)
        return pltpu.make_async_copy(ready_ref.at[part], sums_ref.at[part], sems.at[row])

    for pair_at in range(4):
        lanes = pl.ds(pl.multiple_of(pair_at * 256, 256), 256)
        out_ref[pair_at % 2] = jnp.dot(
            flip_ref[...], left_ref[:, lanes], preferred_element_type=F32
        )
        for half in range(2):
            row = pair_at * 2 + half

            def pack(col_pair, carry):
                for side in range(2):
                    start = pl.multiple_of(col_pair * ROWS + side * COLS, 16)
                    block = out_ref[pair_at % 2, pl.ds(start, COLS), half * LANES : (half + 1) * LANES]
                    rest = block[40:48]
                    head = [
                        jnp.where(
                            lane < 96, block[at * 8 : at * 8 + 8], pltpu.roll(rest, 96 - 32 * at, 1)
                        )
                        for at in range(3)
                    ]
                    whole = jnp.concatenate(head + [block[24:40]], 0)
                    ready_ref[row * 16 + col_pair * 2 + side] = whole.astype(BF16)
                return carry

            lax.fori_loop(0, 8, pack, 0, unroll=8)
            row_copy(row).start()

    for row in range(8):
        row_copy(row).wait()


def triangle(chunks):
    return pl.pallas_call(
        triangle_kernel,
        out_shape=jax.ShapeDtypeStruct((CHANNELS, SUM_ROWS, LANES), BF16),
        in_specs=[pl.BlockSpec(memory_space=pltpu.HBM)],
        out_specs=pl.BlockSpec(memory_space=pltpu.HBM),
        scratch_shapes=[
            pltpu.VMEM((CHANNELS, EDGE_ROWS, LANES), BF16),
            pltpu.VMEM((TOKENS, 1024), BF16),
            pltpu.VMEM((TOKENS, 1024), BF16),
            pltpu.VMEM((TOKENS, TOKENS), BF16),
            pltpu.VMEM((2, TOKENS, 256), F32),
            pltpu.VMEM((CHANNELS, SUM_ROWS, LANES), BF16),
            pltpu.SemaphoreType.DMA((8,)),
            pltpu.SemaphoreType.DMA((8,)),
        ],
        compiler_params=pltpu.CompilerParams(vmem_limit_bytes=52 * 1024 * 1024),
        cost_estimate=pl.CostEstimate(
            flops=2 * 1024 * 1024 * 768, bytes_accessed=4000000, transcendentals=0
        ),
        name="triangle",
    )(chunks)


def update_kernel(
    sums_ref,
    pair_ref,
    gate_ref,
    gain_ref,
    weight_ref,
    out_ref,
    pair_in_ref,
    gate_in_ref,
    ready_ref,
    normed_ref,
    update_ref,
    pair_sems,
    gate_sems,
    out_sems,
):
    parts = [pl.ds(at * 24, 24) for at in range(4)]
    loads = []
    for at, part in enumerate(parts):
        loads.append(
            (
                pltpu.make_async_copy(pair_ref.at[part], pair_in_ref.at[part], pair_sems.at[at]),
                pltpu.make_async_copy(gate_ref.at[part], gate_in_ref.at[part], gate_sems.at[at]),
            )
        )
        for copy in loads[-1]:
            copy.start()
    gain = jnp.broadcast_to(gain_ref[...], (CHANNELS, LANES)).T
    weight = weight_ref[...]

    for step in range(SUM_ROWS // 8):
        tile = sums_ref[:, step * 8 : step * 8 + 8, :].astype(F32)
        center = tile - jnp.mean(tile, 0, keepdims=True)
        scale = lax.rsqrt(jnp.mean(center * center, 0, keepdims=True) + EPSILON)
        normed_ref[...] = (center * scale).reshape(CHANNELS * 8, LANES)
        for at in range(8):
            block = (normed_ref[pl.ds(at, CHANNELS, stride=8), :] * gain).astype(BF16)
            update = lax.dot_general(
                block, weight, (((0,), (0,)), ((), ())), preferred_element_type=F32
            )
            update_ref[pl.ds(step * 8 + at, ROWS, stride=WIDE), :] = update[:ROWS]
            if step < 3:
                start = step * 32 * WIDE + 40 + at
                update_ref[pl.ds(start, 32, stride=WIDE), :] = update[ROWS:]

    stores = []
    for at, part in enumerate(parts):
        for copy in loads[at]:
            copy.wait()
        for step in range(at * 3, at * 3 + 3):
            rows = pl.ds(step * 8, 8)
            update = update_ref[pl.ds(step * 8 * WIDE, 8 * WIDE), :].reshape(8, WIDE, CHANNELS)[:, :COLS]
            ready_ref[rows] = (
                pair_in_ref[rows].astype(F32) + gate_in_ref[rows] * update
            ).astype(BF16)
        copy = pltpu.make_async_copy(ready_ref.at[part], out_ref.at[part], out_sems.at[at])
        copy.start()
        stores.append(copy)
    for copy in stores:
        copy.wait()


def update_pair(sums, pair, gate, out_gain, tri_out):
    far = pl.BlockSpec(memory_space=pltpu.HBM)
    near = pl.BlockSpec(memory_space=pltpu.VMEM)
    return pl.pallas_call(
        update_kernel,
        out_shape=jax.ShapeDtypeStruct((ROWS, COLS, CHANNELS), BF16),
        in_specs=[near, far, far, near, near],
        out_specs=far,
        scratch_shapes=[
            pltpu.VMEM((ROWS, COLS, CHANNELS), BF16),
            pltpu.VMEM((ROWS, COLS, CHANNELS), F32),
            pltpu.VMEM((ROWS, COLS, CHANNELS), BF16),
            pltpu.VMEM((CHANNELS * 8, LANES), F32),
            pltpu.VMEM((ROWS * WIDE, CHANNELS), F32),
            pltpu.SemaphoreType.DMA((4,)),
            pltpu.SemaphoreType.DMA((4,)),
            pltpu.SemaphoreType.DMA((4,)),
        ],
        compiler_params=pltpu.CompilerParams(vmem_limit_bytes=50 * 1024 * 1024),
        cost_estimate=pl.CostEstimate(
            flops=2 * ROWS * COLS * 128 * 128, bytes_accessed=6000000, transcendentals=5000
        ),
        name="update_pair",
    )(sums, pair, gate, out_gain, tri_out)


def split3(values):
    high = values.astype(BF16)
    rest = values - high.astype(F32)
    middle = rest.astype(BF16)
    low = (rest - middle.astype(F32)).astype(BF16)
    return high, middle, low


def side_kernel(
    first_ref, place_ref, pair_ref, gain_ref, weight_ref, bias_ref, gate_ref, band_ref, table_ref
):
    gain = gain_ref[...]
    weight = weight_ref[:, 512:]
    bias = jnp.concatenate([part.astype(F32) for part in split3(bias_ref[...])], 0).astype(BF16)
    table_ref[...] = jnp.zeros_like(table_ref)

    def norm_step(step, carry):
        tile = pair_ref[pl.ds(step * 8, 8)].astype(F32).reshape(8 * COLS, CHANNELS)
        normed = layer_norm(tile)
        inputs = (normed * gain).astype(BF16)
        gate = sigmoid(jnp.dot(inputs, weight, preferred_element_type=F32))
        gate_ref[pl.ds(step * 8, 8)] = gate.reshape(8, COLS, CHANNELS)
        parts = split3(normed)
        for at in range(8):
            rows = slice(at * COLS, (at + 1) * COLS)
            found = sum(
                lax.dot_general(
                    bias, part[rows], (((1,), (1,)), ((), ())), preferred_element_type=F32
                )
                for part in parts
            )
            found = found[0:8] + found[8:16] + found[16:24]
            for head in range(HEADS):
                table_ref[head, pl.ds(8 + step * 8 + at, 1), 0:COLS] = found[head : head + 1]
        return carry

    lax.fori_loop(0, ROWS // 8, norm_step, 0, unroll=4)

    lane = lax.broadcasted_iota(jnp.int32, (BAND_ROWS, LANES), 1)
    row_base = place_ref[0]
    col_base = place_ref[1]

    def band_step(slot, carry):
        first = first_ref[jnp.bitwise_xor(slot, place_ref[2])]
        start = first - row_base + 8
        total = jnp.zeros((BAND_ROWS, LANES), F32)
        shift = col_base - (first - NEAR)
        for head in range(HEADS):
            rows = table_ref[head, pl.ds(start, BAND_ROWS), :]
            moved = pltpu.roll(rows, lax.rem(shift + head * BAND_COLS + 16 * LANES, LANES), 1)
            col = lane - head * BAND_COLS - shift
            keep = (lane // BAND_COLS == head) & (col >= 0) & (col < COLS)
            total = total + jnp.where(keep, moved, 0.0)
        band_ref[slot] = total
        return carry

    lax.fori_loop(0, 16, band_step, 0, unroll=4)


def side(first, place, pair, pair_gain, gate_weight, bias_wide):
    whole = pl.BlockSpec(memory_space=pltpu.VMEM)
    scalars = pl.BlockSpec(memory_space=pltpu.SMEM)
    return pl.pallas_call(
        side_kernel,
        out_shape=(
            jax.ShapeDtypeStruct((ROWS, COLS, CHANNELS), F32),
            jax.ShapeDtypeStruct((16, BAND_ROWS, LANES), F32),
        ),
        in_specs=[scalars, scalars, whole, whole, whole, whole],
        out_specs=(whole, whole),
        scratch_shapes=[pltpu.VMEM((HEADS, ROWS + 32, LANES), F32)],
        compiler_params=pltpu.CompilerParams(vmem_limit_bytes=VMEM_LIMIT),
        cost_estimate=pl.CostEstimate(
            flops=8 * ROWS * COLS * 128 * 128, bytes_accessed=5000000, transcendentals=600000
        ),
        name="side",
    )(first, place, pair, pair_gain, gate_weight, bias_wide)


def atoms_kernel(
    base_ref,
    atoms_ref,
    before_ref,
    after_ref,
    band0_ref,
    band1_ref,
    band2_ref,
    band3_ref,
    lane_start_ref,
    lane_end_ref,
    sub_start_ref,
    sub_end_ref,
    gain_ref,
    project_ref,
    output_ref,
    trans_gain_ref,
    up_ref,
    down_ref,
    out_ref,
):
    base = base_ref[0]
    own = atoms_ref[...].astype(F32)
    around = jnp.concatenate(
        [before_ref[...].astype(F32), own, after_ref[...].astype(F32)], 0
    )
    inputs = (layer_norm(around) * gain_ref[...]).astype(BF16)
    projected = jnp.dot(inputs, project_ref[...], preferred_element_type=F32)
    query = projected[HALO : HALO + ATOM_ROWS, 0:128].astype(BF16)
    key = projected[:, 128:256].astype(BF16)
    value = projected[:, 256:384].astype(BF16)
    gate = projected[HALO : HALO + ATOM_ROWS, 384:512].astype(BF16).astype(F32)

    query_atom = base + lax.broadcasted_iota(jnp.int32, (ATOM_ROWS, LANES), 0)
    query_hot = (
        ((query_atom >= lane_start_ref[...]) & (query_atom < lane_end_ref[...]))
        .astype(F32)
        .astype(BF16)
    )
    key_atom = base - HALO + lax.broadcasted_iota(jnp.int32, (LANES, KEY_ROWS), 1)
    key_hot = (
        ((key_atom >= sub_start_ref[...]) & (key_atom < sub_end_ref[...])).astype(F32)
    )
    token_head = lax.broadcasted_iota(jnp.int32, (LANES, KEY_ROWS), 0) // BAND_COLS

    band = band0_ref[0] + band1_ref[0] + band2_ref[0] + band3_ref[0]
    band = jnp.concatenate([band, jnp.zeros((LANES - BAND_ROWS, LANES), F32)], 0)
    picked = [
        jnp.dot(query_hot, part, preferred_element_type=F32).astype(BF16) for part in split3(band)
    ]

    window = lax.broadcasted_iota(jnp.int32, (ATOM_ROWS, KEY_ROWS), 0) // QUERIES
    place = lax.broadcasted_iota(jnp.int32, (ATOM_ROWS, KEY_ROWS), 1)
    near = place - window * QUERIES
    atom = base - HALO + place
    allowed = (near >= 0) & (near < KEYS) & (atom >= 0) & (atom < TOKENS * 32)
    lane_head = lax.broadcasted_iota(jnp.int32, (ATOM_ROWS, LANES), 1) // HEAD_DIM
    mixed = jnp.zeros((ATOM_ROWS, LANES), F32)
    for head in range(HEADS):
        own_query = jnp.where(lane_head == head, query.astype(F32), 0.0).astype(BF16)
        scores = lax.dot_general(
            own_query, key, (((1,), (1,)), ((), ())), preferred_element_type=F32
        ) * (HEAD_DIM**-0.5)
        head_hot = jnp.where(token_head == head, key_hot, 0.0).astype(BF16)
        for part in picked:
            scores = scores + jnp.dot(part, head_hot, preferred_element_type=F32)
        scores = jnp.where(allowed, scores, -jnp.inf)
        grown = jnp.exp(scores - jnp.max(scores, -1, keepdims=True))
        weights = (grown / jnp.sum(grown, -1, keepdims=True)).astype(BF16)
        mixed = mixed + jnp.where(
            lane_head == head, jnp.dot(weights, value, preferred_element_type=F32), 0.0
        )
    attended = (mixed * sigmoid(gate)).astype(BF16)
    state = own + jnp.dot(attended, output_ref[...], preferred_element_type=F32)
    inner = (layer_norm(state) * trans_gain_ref[...]).astype(BF16)
    upward = jnp.dot(inner, up_ref[...], preferred_element_type=F32)
    first, second = upward[:, :256], upward[:, 256:]
    hidden = (first * sigmoid(first) * second).astype(BF16)
    out_ref[...] = (
        state + jnp.dot(hidden, down_ref[...], preferred_element_type=F32)
    ).astype(BF16)


def atoms_block(base, *arrays):
    whole = pl.BlockSpec(memory_space=pltpu.VMEM)
    return pl.pallas_call(
        atoms_kernel,
        out_shape=jax.ShapeDtypeStruct((ATOM_ROWS, LANES), BF16),
        in_specs=[pl.BlockSpec(memory_space=pltpu.SMEM)] + [whole] * len(arrays),
        out_specs=whole,
        compiler_params=pltpu.CompilerParams(vmem_limit_bytes=VMEM_LIMIT),
        cost_estimate=pl.CostEstimate(
            flops=2 * 400 * 1000 * 1000, bytes_accessed=2000000, transcendentals=400000
        ),
        name="atoms_block",
    )(base, *arrays)


def on_device(
    pair,
    atoms,
    token_atoms,
    pair_gain,
    tri_proj,
    tri_out,
    out_gain,
    bias_weight,
    atom_gain,
    atom_proj,
    atom_out,
    trans_gain,
    trans_up,
    trans_down,
):
    row_id = lax.axis_index("row")
    col_id = lax.axis_index("col")
    device = row_id * 16 + col_id

    chunks, later_gain = edges(pair, pair_gain[None], tri_proj)
    arrived = lax.all_to_all(chunks, BOTH, 0, 0, tiled=True)

    ends = jnp.cumsum(token_atoms)
    starts = ends - token_atoms
    firsts_at = (row_id * 16 + jnp.arange(16, dtype=jnp.int32)) * ATOM_ROWS
    firsts = jnp.sum((ends[None, :] <= firsts_at[:, None]).astype(jnp.int32), 1)
    first = jnp.sum((ends <= device * ATOM_ROWS).astype(jnp.int32))
    far = jnp.full((LANES,), -1, jnp.int32)
    all_starts = jnp.concatenate([far, starts, far])
    all_ends = jnp.concatenate([far, ends, far])
    lane_start = lax.dynamic_slice(all_starts, (first + LANES,), (LANES,))
    lane_end = lax.dynamic_slice(all_ends, (first + LANES,), (LANES,))
    sub_start = lax.dynamic_slice(all_starts, (first + LANES - NEAR,), (BAND_COLS,))
    sub_end = lax.dynamic_slice(all_ends, (first + LANES - NEAR,), (BAND_COLS,))

    bias_wide = jnp.pad(bias_weight.T, ((0, 4), (0, 0)))
    place = jnp.stack([row_id * ROWS, col_id * COLS, col_id]).astype(jnp.int32)
    gate, bands = side(firsts, place, pair, later_gain, tri_proj, bias_wide)
    def exchange(values, size):
        parts = [values[:size]]
        for at in range(1, 4):
            pairs = [(device, device ^ (at * size)) for device in range(16)]
            parts.append(lax.ppermute(values[at * size : (at + 1) * size], "col", pairs))
        return parts

    halves = exchange(bands, 4)
    ring = list(range(127))
    before = lax.ppermute(atoms[ATOM_ROWS - HALO :], BOTH, [(at, at + 1) for at in ring])
    after = lax.ppermute(atoms[:HALO], BOTH, [(at + 1, at) for at in ring])
    arrived, before, after, *halves = lax.optimization_barrier(
        (arrived, before, after, *halves)
    )
    parts = exchange(sum(halves), 1)
    atoms_out = atoms_block(
        (device * ATOM_ROWS).astype(jnp.int32)[None],
        atoms,
        before,
        after,
        *parts,
        lane_start[None],
        lane_end[None],
        jnp.tile(sub_start, HEADS)[:, None],
        jnp.tile(sub_end, HEADS)[:, None],
        atom_gain[None],
        atom_proj,
        atom_out,
        trans_gain[None],
        trans_up,
        trans_down,
    )

    sums = triangle(arrived)
    returned = lax.all_to_all(sums, BOTH, 0, 0, tiled=True)
    pair_out = update_pair(returned, pair, gate, out_gain[None], tri_out)
    return (pair_out, atoms_out)


def solution(mesh):
    return jax.shard_map(
        on_device,
        mesh=mesh,
        in_specs=(P("row", "col", None), P(BOTH, None)) + (P(),) * 12,
        out_specs=(P("row", "col", None), P(BOTH, None)),
        check_vma=False,
    )
```

```python
import functools

import jax
import jax.numpy as jnp
from jax import lax
from jax.experimental import pallas as pl
from jax.experimental.pallas import tpu as pltpu
from jax.sharding import PartitionSpec as P

ROWS = 96
COLS = 48
LANES = 128
CHANNELS = 128
TOKENS = 768
QUERIES = 32
KEYS = 128
HALO = 48
ATOM_ROWS = 192
KEY_ROWS = ATOM_ROWS + 2 * HALO
HEADS = 4
HEAD_DIM = 32
NEAR = 5
BAND_ROWS = 16
BAND_COLS = 32
EDGE_ROWS = 72
WIDE = 56
SUM_ROWS = 36
SUM_TILES = CHANNELS * SUM_ROWS // 8
EPSILON = 1e-05
BOTH = ("row", "col")
VMEM_LIMIT = 20 * 1024 * 1024

F32 = jnp.float32
BF16 = jnp.bfloat16


def layer_norm(values):
    center = values - jnp.mean(values, -1, keepdims=True)
    return center * lax.rsqrt(jnp.mean(center * center, -1, keepdims=True) + EPSILON)


def sigmoid(values):
    return 0.5 * jnp.tanh(0.5 * values) + 0.5


def edges_kernel(
    pair_ref,
    gain_ref,
    weight_ref,
    edges_ref,
    gain_out_ref,
    tile_ref,
    gain_in_ref,
    weight_in_ref,
    wide_ref,
    stage_ref,
    ready_ref,
    in_sems,
    param_sems,
    out_sems,
):
    steps = ROWS // 8
    gain_copy = pltpu.make_async_copy(gain_ref, gain_in_ref, param_sems.at[0])
    weight_copy = pltpu.make_async_copy(weight_ref, weight_in_ref, param_sems.at[1])
    tile_copies = [
        pltpu.make_async_copy(
            pair_ref.at[pl.ds(step * 8, 8)], tile_ref.at[pl.ds(step * 8, 8)], in_sems.at[step]
        )
        for step in range(steps)
    ]
    gain_copy.start()
    for copy in tile_copies:
        copy.start()
    weight_copy.start()
    gain_copy.wait()
    gain_out_ref[...] = gain_in_ref[...]
    gain = jnp.broadcast_to(gain_in_ref[...], (2 * LANES, CHANNELS)).T
    eye = (
        lax.broadcasted_iota(jnp.int32, (CHANNELS, CHANNELS), 0)
        == lax.broadcasted_iota(jnp.int32, (CHANNELS, CHANNELS), 1)
    ).astype(F32).astype(BF16)

    def norm_step(step, carry):
        rows = pl.ds(step * 8, 8)
        pltpu.make_async_copy(pair_ref.at[rows], tile_ref.at[rows], in_sems.at[step]).wait()
        tile = tile_ref[rows].astype(F32)
        for at in range(8):
            start = pl.multiple_of((step * 8 + at) * WIDE, 8)
            wide_ref[pl.ds(start, COLS), :] = tile[at]
        return carry

    lax.fori_loop(0, steps, norm_step, 0, unroll=3)
    weight_copy.wait()
    weight = weight_in_ref[:, :512].T

    def packed(col, third, extra):
        main = wide_ref[pl.ds(col, ROWS, stride=WIDE), :]
        rest = wide_ref[pl.ds(third * 32 * WIDE + extra, 32, stride=WIDE), :]
        return jnp.concatenate([main, rest], 0).astype(BF16)

    def emit(sources, count):
        for at in range(0, count, 2):
            rows = jnp.concatenate([packed(*source) for source in sources[at : at + 2]], 0)
            flipped = lax.dot_general(
                eye, rows, (((1,), (1,)), ((), ())), preferred_element_type=F32
            )
            center = flipped - jnp.mean(flipped, 0, keepdims=True)
            scale = lax.rsqrt(jnp.mean(center * center, 0, keepdims=True) + EPSILON)
            inputs = (center * scale * gain).astype(BF16)
            project = jnp.dot(weight, inputs, preferred_element_type=F32)
            left = sigmoid(project[:128]) * project[128:256]
            right = sigmoid(project[256:384]) * project[384:]
            for half in range(2):
                lanes = slice(half * LANES, (half + 1) * LANES)
                stage_ref[pl.ds(at + half, CHANNELS, stride=24), :] = left[:, lanes]
                stage_ref[pl.ds(count + at + half, CHANNELS, stride=24), :] = right[:, lanes]

    def block_copy(group):
        rows = pl.ds(pl.multiple_of(group * 16, 16), 16)
        return pltpu.make_async_copy(
            ready_ref.at[group], edges_ref.at[:, rows, :], out_sems.at[group]
        )

    def block(group, carry):
        sources = []
        for at in range(8):
            third = jnp.where(group < 3, group, at // 4)
            extra = jnp.where(group < 3, 36 + at, 44 + at % 4)
            sources.append((group * 8 + at, third, extra))
        emit(sources, 8)
        ready_ref[group] = stage_ref[...].reshape(CHANNELS, 24, LANES)[:, :16].astype(BF16)
        block_copy(group).start()
        return carry

    lax.fori_loop(0, 4, block, 0, unroll=4)
    emit([(32 + at, 2, 44 + at) for at in range(4)], 4)
    ready_ref[4, :, 0:8, :] = stage_ref[...].reshape(CHANNELS, 24, LANES)[:, :8].astype(BF16)
    last = pltpu.make_async_copy(
        ready_ref.at[4, :, pl.ds(0, 8), :], edges_ref.at[:, pl.ds(64, 8), :], out_sems.at[4]
    )
    last.start()
    for group in range(4):
        block_copy(group).wait()
    last.wait()


def edges(pair, pair_gain, weight):
    far = pl.BlockSpec(memory_space=pltpu.HBM)
    return pl.pallas_call(
        edges_kernel,
        out_shape=(
            jax.ShapeDtypeStruct((CHANNELS, EDGE_ROWS, LANES), BF16),
            jax.ShapeDtypeStruct((1, CHANNELS), F32),
        ),
        in_specs=[far] * 3,
        out_specs=(far, pl.BlockSpec(memory_space=pltpu.VMEM)),
        scratch_shapes=[
            pltpu.VMEM((ROWS, COLS, CHANNELS), BF16),
            pltpu.VMEM((1, CHANNELS), F32),
            pltpu.VMEM((CHANNELS, 640), BF16),
            pltpu.VMEM((ROWS * WIDE, CHANNELS), F32),
            pltpu.VMEM((CHANNELS * 24, LANES), F32),
            pltpu.VMEM((5, CHANNELS, 16, LANES), BF16),
            pltpu.SemaphoreType.DMA((ROWS // 8,)),
            pltpu.SemaphoreType.DMA((2,)),
            pltpu.SemaphoreType.DMA((5,)),
        ],
        compiler_params=pltpu.CompilerParams(vmem_limit_bytes=56 * 1024 * 1024),
        cost_estimate=pl.CostEstimate(
            flops=2 * ROWS * COLS * 128 * 512, bytes_accessed=4000000, transcendentals=1200000
        ),
        name="edges",
    )(pair, pair_gain, weight)


def triangle_kernel(
    arrived_ref,
    sums_ref,
    chunks_ref,
    left_ref,
    right_ref,
    flip_ref,
    out_ref,
    ready_ref,
    in_sems,
    sems,
):
    def row_load(row):
        part = pl.ds(pl.multiple_of(row * 16, 16), 16)
        return pltpu.make_async_copy(arrived_ref.at[part], chunks_ref.at[part], in_sems.at[row])

    for row in range(8):
        row_load(row).start()

    lane = lax.broadcasted_iota(jnp.int32, (8, LANES), 1)
    low = lax.broadcasted_iota(jnp.int32, (8, LANES), 0) < 4

    def thirds(first, second, third):
        return jnp.where(
            lane < 32,
            pltpu.roll(first, 32, 1),
            jnp.where(lane < 64, pltpu.roll(second, 64, 1), pltpu.roll(third, 96, 1)),
        )

    def gather_row(row, carry):
        row_load(row).wait()
        lanes = pl.ds(pl.multiple_of(row * LANES, LANES), LANES)

        def gather(col, carry):
            chunk = chunks_ref[row * 16 + col].astype(F32)
            part = [chunk[at * 8 : at * 8 + 8] for at in range(9)]
            tail = part[8]
            turned = pltpu.roll(tail, 4, 0)
            at_rows = pl.ds(pl.multiple_of(col * COLS, COLS), COLS)
            left, right = part[0:8:2], part[1:8:2]
            for ref, main, last, spare in (
                (left_ref, left, tail, turned),
                (right_ref, right, turned, tail),
            ):
                fine = thirds(pltpu.roll(main[3], 4, 0), main[3], spare)
                whole = jnp.concatenate(
                    main + [thirds(main[0], main[1], main[2]), jnp.where(low, last, fine)], 0
                )
                ref[at_rows, lanes] = whole.astype(BF16)
            return carry

        lax.fori_loop(0, 16, gather, 0, unroll=16)
        flip_ref[pl.ds(pl.multiple_of(row * ROWS, ROWS), ROWS), :] = right_ref[:, lanes].T[:ROWS]
        return carry

    lax.fori_loop(0, 8, gather_row, 0, unroll=True)

    def row_copy(row):
        part = pl.ds(row * 72, 72)
        return pltpu.make_async_copy(ready_ref.at[part], sums_ref.at[part], sems.at[row])

    for pair_at in range(4):
        lanes = pl.ds(pl.multiple_of(pair_at * 256, 256), 256)
        out_ref[pair_at % 2] = jnp.dot(
            flip_ref[...], left_ref[:, lanes], preferred_element_type=F32
        )
        for half in range(2):
            row = pair_at * 2 + half

            def pack(col_pair, carry):
                tiles = []
                for side in range(2):
                    start = pl.multiple_of(col_pair * ROWS + side * COLS, 16)
                    block = out_ref[
                        pair_at % 2, pl.ds(start, COLS), half * LANES : (half + 1) * LANES
                    ]
                    part = [block[at * 8 : at * 8 + 8] for at in range(6)]
                    turned = pltpu.roll(part[4], 4, 0)
                    fine = jnp.where(low, pltpu.roll(turned, 96, 1), pltpu.roll(part[4], 64, 1))
                    rest = [pltpu.roll(part[5], 96 - 32 * at, 1) for at in range(3)] + [fine]
                    whole = [jnp.where(lane < 96, part[at], rest[at]) for at in range(4)]
                    if side == 0:
                        last = jnp.where(lane < 96, part[4], pltpu.roll(turned, 32, 1))
                        tiles = whole
                    else:
                        other = jnp.where(lane < 96, turned, pltpu.roll(part[4], 32, 1))
                        tiles = tiles + [jnp.where(low, last, other)] + whole
                packed = jnp.concatenate(tiles, 0).reshape(9, 8, LANES).astype(BF16)
                ready_ref[pl.ds((row * 8 + col_pair) * 9, 9)] = packed
                return carry

            lax.fori_loop(0, 8, pack, 0, unroll=8)
            row_copy(row).start()

    for row in range(8):
        row_copy(row).wait()


def triangle(chunks):
    return pl.pallas_call(
        triangle_kernel,
        out_shape=jax.ShapeDtypeStruct((SUM_TILES, 8, LANES), BF16),
        in_specs=[pl.BlockSpec(memory_space=pltpu.HBM)],
        out_specs=pl.BlockSpec(memory_space=pltpu.HBM),
        scratch_shapes=[
            pltpu.VMEM((CHANNELS, EDGE_ROWS, LANES), BF16),
            pltpu.VMEM((TOKENS, 1024), BF16),
            pltpu.VMEM((TOKENS, 1024), BF16),
            pltpu.VMEM((TOKENS, TOKENS), BF16),
            pltpu.VMEM((2, TOKENS, 256), F32),
            pltpu.VMEM((SUM_TILES, 8, LANES), BF16),
            pltpu.SemaphoreType.DMA((8,)),
            pltpu.SemaphoreType.DMA((8,)),
        ],
        compiler_params=pltpu.CompilerParams(vmem_limit_bytes=52 * 1024 * 1024),
        cost_estimate=pl.CostEstimate(
            flops=2 * 1024 * 1024 * 768, bytes_accessed=4000000, transcendentals=0
        ),
        name="triangle",
    )(chunks)


def update_kernel(
    odd_ref,
    sums_ref,
    pair_ref,
    gate_ref,
    gain_ref,
    weight_ref,
    out_ref,
    pair_in_ref,
    gate_in_ref,
    ready_ref,
    normed_ref,
    fold_ref,
    update_ref,
    pair_sems,
    gate_sems,
    out_sems,
):
    parts = [pl.ds(at * 24, 24) for at in range(4)]
    loads = []
    for at, part in enumerate(parts):
        loads.append(
            (
                pltpu.make_async_copy(pair_ref.at[part], pair_in_ref.at[part], pair_sems.at[at]),
                pltpu.make_async_copy(gate_ref.at[part], gate_in_ref.at[part], gate_sems.at[at]),
            )
        )
        for copy in loads[-1]:
            copy.start()
    gain = jnp.broadcast_to(gain_ref[...], (CHANNELS, LANES)).T
    weight = weight_ref[...]

    def tiles(step):
        return sums_ref[step * 72 : step * 72 + 72].astype(F32).reshape(8, 9, 8, LANES)

    def channel_mean(total):
        fold_ref[...] = total.reshape(2 * SUM_ROWS, LANES)
        mean = (fold_ref[0:SUM_ROWS] + fold_ref[SUM_ROWS:]) * (1.0 / CHANNELS)
        fold_ref[0:SUM_ROWS] = mean
        fold_ref[SUM_ROWS:] = mean
        return fold_ref[...].reshape(1, 9, 8, LANES)

    total = jnp.zeros((9, 8, LANES), F32)
    for step in range(8):
        total = total + jnp.sum(tiles(step), 0)
    mean = channel_mean(total)
    total = jnp.zeros((9, 8, LANES), F32)
    for step in range(8):
        center = tiles(step) - mean
        total = total + jnp.sum(center * center, 0)
    scale = lax.rsqrt(channel_mean(total) + EPSILON)
    for step in range(8):
        normed = (tiles(step) - mean) * scale
        normed_ref[step * 576 : step * 576 + 576, :] = normed.reshape(576, LANES)

    turn = odd_ref[0] * 4
    for at in range(SUM_ROWS):
        row = lax.rem(turn + at, SUM_ROWS)
        block = (normed_ref[pl.ds(row, CHANNELS, stride=SUM_ROWS), :] * gain).astype(BF16)
        update = lax.dot_general(
            block, weight, (((0,), (0,)), ((), ())), preferred_element_type=F32
        )
        update_ref[pl.ds(at, ROWS, stride=WIDE), :] = update[:ROWS]
        third, col = (at // 8, 40 + at % 8) if at < 24 else (at // 4 - 6, 36 + at % 4)
        update_ref[pl.ds(third * 32 * WIDE + col, 32, stride=WIDE), :] = update[ROWS:]

    stores = []
    for at, part in enumerate(parts):
        for copy in loads[at]:
            copy.wait()
        for step in range(at * 3, at * 3 + 3):
            rows = pl.ds(step * 8, 8)
            update = update_ref[pl.ds(step * 8 * WIDE, 8 * WIDE), :].reshape(8, WIDE, CHANNELS)[:, :COLS]
            ready_ref[rows] = (
                pair_in_ref[rows].astype(F32) + gate_in_ref[rows] * update
            ).astype(BF16)
        copy = pltpu.make_async_copy(ready_ref.at[part], out_ref.at[part], out_sems.at[at])
        copy.start()
        stores.append(copy)
    for copy in stores:
        copy.wait()


def update_pair(odd, sums, pair, gate, out_gain, tri_out):
    far = pl.BlockSpec(memory_space=pltpu.HBM)
    near = pl.BlockSpec(memory_space=pltpu.VMEM)
    return pl.pallas_call(
        update_kernel,
        out_shape=jax.ShapeDtypeStruct((ROWS, COLS, CHANNELS), BF16),
        in_specs=[pl.BlockSpec(memory_space=pltpu.SMEM), near, far, far, near, near],
        out_specs=far,
        scratch_shapes=[
            pltpu.VMEM((ROWS, COLS, CHANNELS), BF16),
            pltpu.VMEM((ROWS, COLS, CHANNELS), F32),
            pltpu.VMEM((ROWS, COLS, CHANNELS), BF16),
            pltpu.VMEM((CHANNELS * SUM_ROWS, LANES), F32),
            pltpu.VMEM((2 * SUM_ROWS, LANES), F32),
            pltpu.VMEM((ROWS * WIDE, CHANNELS), F32),
            pltpu.SemaphoreType.DMA((4,)),
            pltpu.SemaphoreType.DMA((4,)),
            pltpu.SemaphoreType.DMA((4,)),
        ],
        compiler_params=pltpu.CompilerParams(vmem_limit_bytes=50 * 1024 * 1024),
        cost_estimate=pl.CostEstimate(
            flops=2 * ROWS * COLS * 128 * 128, bytes_accessed=6000000, transcendentals=5000
        ),
        name="update_pair",
    )(odd, sums, pair, gate, out_gain, tri_out)


def split3(values):
    high = values.astype(BF16)
    rest = values - high.astype(F32)
    middle = rest.astype(BF16)
    low = (rest - middle.astype(F32)).astype(BF16)
    return high, middle, low


def side_kernel(
    first_ref, place_ref, pair_ref, gain_ref, weight_ref, bias_ref, gate_ref, band_ref, table_ref
):
    gain = gain_ref[...]
    weight = weight_ref[:, 512:]
    bias = jnp.concatenate([part.astype(F32) for part in split3(bias_ref[...])], 0).astype(BF16)
    table_ref[...] = jnp.zeros_like(table_ref)

    def norm_step(step, carry):
        tile = pair_ref[pl.ds(step * 8, 8)].astype(F32).reshape(8 * COLS, CHANNELS)
        normed = layer_norm(tile)
        inputs = (normed * gain).astype(BF16)
        gate = sigmoid(jnp.dot(inputs, weight, preferred_element_type=F32))
        gate_ref[pl.ds(step * 8, 8)] = gate.reshape(8, COLS, CHANNELS)
        parts = split3(normed)
        for at in range(8):
            rows = slice(at * COLS, (at + 1) * COLS)
            found = sum(
                lax.dot_general(
                    bias, part[rows], (((1,), (1,)), ((), ())), preferred_element_type=F32
                )
                for part in parts
            )
            found = found[0:8] + found[8:16] + found[16:24]
            for head in range(HEADS):
                table_ref[head, pl.ds(8 + step * 8 + at, 1), 0:COLS] = found[head : head + 1]
        return carry

    lax.fori_loop(0, ROWS // 8, norm_step, 0, unroll=4)

    lane = lax.broadcasted_iota(jnp.int32, (BAND_ROWS, LANES), 1)
    row_base = place_ref[0]
    col_base = place_ref[1]

    def band_step(slot, carry):
        first = first_ref[jnp.bitwise_xor(slot, place_ref[2])]
        start = first - row_base + 8
        total = jnp.zeros((BAND_ROWS, LANES), F32)
        shift = col_base - (first - NEAR)
        for head in range(HEADS):
            rows = table_ref[head, pl.ds(start, BAND_ROWS), :]
            moved = pltpu.roll(rows, lax.rem(shift + head * BAND_COLS + 16 * LANES, LANES), 1)
            col = lane - head * BAND_COLS - shift
            keep = (lane // BAND_COLS == head) & (col >= 0) & (col < COLS)
            total = total + jnp.where(keep, moved, 0.0)
        band_ref[slot] = total
        return carry

    lax.fori_loop(0, 16, band_step, 0, unroll=4)


def side(first, place, pair, pair_gain, gate_weight, bias_wide):
    whole = pl.BlockSpec(memory_space=pltpu.VMEM)
    scalars = pl.BlockSpec(memory_space=pltpu.SMEM)
    return pl.pallas_call(
        side_kernel,
        out_shape=(
            jax.ShapeDtypeStruct((ROWS, COLS, CHANNELS), F32),
            jax.ShapeDtypeStruct((16, BAND_ROWS, LANES), F32),
        ),
        in_specs=[scalars, scalars, whole, whole, whole, whole],
        out_specs=(whole, whole),
        scratch_shapes=[pltpu.VMEM((HEADS, ROWS + 32, LANES), F32)],
        compiler_params=pltpu.CompilerParams(vmem_limit_bytes=VMEM_LIMIT),
        cost_estimate=pl.CostEstimate(
            flops=8 * ROWS * COLS * 128 * 128, bytes_accessed=5000000, transcendentals=600000
        ),
        name="side",
    )(first, place, pair, pair_gain, gate_weight, bias_wide)


def atoms_kernel(
    base_ref,
    atoms_ref,
    before_ref,
    after_ref,
    band0_ref,
    band1_ref,
    band2_ref,
    band3_ref,
    lane_start_ref,
    lane_end_ref,
    sub_start_ref,
    sub_end_ref,
    gain_ref,
    project_ref,
    output_ref,
    trans_gain_ref,
    up_ref,
    down_ref,
    out_ref,
):
    base = base_ref[0]
    own = atoms_ref[...].astype(F32)
    around = jnp.concatenate(
        [before_ref[...].astype(F32), own, after_ref[...].astype(F32)], 0
    )
    inputs = (layer_norm(around) * gain_ref[...]).astype(BF16)
    projected = jnp.dot(inputs, project_ref[...], preferred_element_type=F32)
    query = projected[HALO : HALO + ATOM_ROWS, 0:128].astype(BF16)
    key = projected[:, 128:256].astype(BF16)
    value = projected[:, 256:384].astype(BF16)
    gate = projected[HALO : HALO + ATOM_ROWS, 384:512].astype(BF16).astype(F32)

    query_atom = base + lax.broadcasted_iota(jnp.int32, (ATOM_ROWS, LANES), 0)
    query_hot = (
        ((query_atom >= lane_start_ref[...]) & (query_atom < lane_end_ref[...]))
        .astype(F32)
        .astype(BF16)
    )
    key_atom = base - HALO + lax.broadcasted_iota(jnp.int32, (LANES, KEY_ROWS), 1)
    key_hot = (
        ((key_atom >= sub_start_ref[...]) & (key_atom < sub_end_ref[...])).astype(F32)
    )
    token_head = lax.broadcasted_iota(jnp.int32, (LANES, KEY_ROWS), 0) // BAND_COLS

    band = band0_ref[0] + band1_ref[0] + band2_ref[0] + band3_ref[0]
    band = jnp.concatenate([band, jnp.zeros((LANES - BAND_ROWS, LANES), F32)], 0)
    picked = [
        jnp.dot(query_hot, part, preferred_element_type=F32).astype(BF16) for part in split3(band)
    ]

    window = lax.broadcasted_iota(jnp.int32, (ATOM_ROWS, KEY_ROWS), 0) // QUERIES
    place = lax.broadcasted_iota(jnp.int32, (ATOM_ROWS, KEY_ROWS), 1)
    near = place - window * QUERIES
    atom = base - HALO + place
    allowed = (near >= 0) & (near < KEYS) & (atom >= 0) & (atom < TOKENS * 32)
    lane_head = lax.broadcasted_iota(jnp.int32, (ATOM_ROWS, LANES), 1) // HEAD_DIM
    mixed = jnp.zeros((ATOM_ROWS, LANES), F32)
    for head in range(HEADS):
        own_query = jnp.where(lane_head == head, query.astype(F32), 0.0).astype(BF16)
        scores = lax.dot_general(
            own_query, key, (((1,), (1,)), ((), ())), preferred_element_type=F32
        ) * (HEAD_DIM**-0.5)
        head_hot = jnp.where(token_head == head, key_hot, 0.0).astype(BF16)
        for part in picked:
            scores = scores + jnp.dot(part, head_hot, preferred_element_type=F32)
        scores = jnp.where(allowed, scores, -jnp.inf)
        grown = jnp.exp(scores - jnp.max(scores, -1, keepdims=True))
        weights = (grown / jnp.sum(grown, -1, keepdims=True)).astype(BF16)
        mixed = mixed + jnp.where(
            lane_head == head, jnp.dot(weights, value, preferred_element_type=F32), 0.0
        )
    attended = (mixed * sigmoid(gate)).astype(BF16)
    state = own + jnp.dot(attended, output_ref[...], preferred_element_type=F32)
    inner = (layer_norm(state) * trans_gain_ref[...]).astype(BF16)
    upward = jnp.dot(inner, up_ref[...], preferred_element_type=F32)
    first, second = upward[:, :256], upward[:, 256:]
    hidden = (first * sigmoid(first) * second).astype(BF16)
    out_ref[...] = (
        state + jnp.dot(hidden, down_ref[...], preferred_element_type=F32)
    ).astype(BF16)


def atoms_block(base, *arrays):
    whole = pl.BlockSpec(memory_space=pltpu.VMEM)
    return pl.pallas_call(
        atoms_kernel,
        out_shape=jax.ShapeDtypeStruct((ATOM_ROWS, LANES), BF16),
        in_specs=[pl.BlockSpec(memory_space=pltpu.SMEM)] + [whole] * len(arrays),
        out_specs=whole,
        compiler_params=pltpu.CompilerParams(vmem_limit_bytes=VMEM_LIMIT),
        cost_estimate=pl.CostEstimate(
            flops=2 * 400 * 1000 * 1000, bytes_accessed=2000000, transcendentals=400000
        ),
        name="atoms_block",
    )(base, *arrays)


def on_device(
    pair,
    atoms,
    token_atoms,
    pair_gain,
    tri_proj,
    tri_out,
    out_gain,
    bias_weight,
    atom_gain,
    atom_proj,
    atom_out,
    trans_gain,
    trans_up,
    trans_down,
):
    row_id = lax.axis_index("row")
    col_id = lax.axis_index("col")
    device = row_id * 16 + col_id

    chunks, later_gain = edges(pair, pair_gain[None], tri_proj)
    arrived = lax.all_to_all(chunks, BOTH, 0, 0, tiled=True)

    ends = jnp.cumsum(token_atoms)
    starts = ends - token_atoms
    firsts_at = (row_id * 16 + jnp.arange(16, dtype=jnp.int32)) * ATOM_ROWS
    firsts = jnp.sum((ends[None, :] <= firsts_at[:, None]).astype(jnp.int32), 1)
    first = jnp.sum((ends <= device * ATOM_ROWS).astype(jnp.int32))
    far = jnp.full((LANES,), -1, jnp.int32)
    all_starts = jnp.concatenate([far, starts, far])
    all_ends = jnp.concatenate([far, ends, far])
    lane_start = lax.dynamic_slice(all_starts, (first + LANES,), (LANES,))
    lane_end = lax.dynamic_slice(all_ends, (first + LANES,), (LANES,))
    sub_start = lax.dynamic_slice(all_starts, (first + LANES - NEAR,), (BAND_COLS,))
    sub_end = lax.dynamic_slice(all_ends, (first + LANES - NEAR,), (BAND_COLS,))

    bias_wide = jnp.pad(bias_weight.T, ((0, 4), (0, 0)))
    place = jnp.stack([row_id * ROWS, col_id * COLS, col_id]).astype(jnp.int32)
    gate, bands = side(firsts, place, pair, later_gain, tri_proj, bias_wide)
    def exchange(values, size):
        parts = [values[:size]]
        for at in range(1, 4):
            pairs = [(device, device ^ (at * size)) for device in range(16)]
            parts.append(lax.ppermute(values[at * size : (at + 1) * size], "col", pairs))
        return parts

    halves = exchange(bands, 4)
    ring = list(range(127))
    before = lax.ppermute(atoms[ATOM_ROWS - HALO :], BOTH, [(at, at + 1) for at in ring])
    after = lax.ppermute(atoms[:HALO], BOTH, [(at + 1, at) for at in ring])
    arrived, before, after, *halves = lax.optimization_barrier(
        (arrived, before, after, *halves)
    )
    parts = exchange(sum(halves), 1)
    atoms_out = atoms_block(
        (device * ATOM_ROWS).astype(jnp.int32)[None],
        atoms,
        before,
        after,
        *parts,
        lane_start[None],
        lane_end[None],
        jnp.tile(sub_start, HEADS)[:, None],
        jnp.tile(sub_end, HEADS)[:, None],
        atom_gain[None],
        atom_proj,
        atom_out,
        trans_gain[None],
        trans_up,
        trans_down,
    )

    sums = triangle(arrived)
    chunks = sums.reshape(CHANNELS, SUM_ROWS // 4, 4, LANES)
    returned = lax.all_to_all(chunks, BOTH, 0, 0, tiled=True).reshape(sums.shape)
    odd = lax.rem(col_id, 2).astype(jnp.int32)[None]
    pair_out = update_pair(odd, returned, pair, gate, out_gain[None], tri_out)
    return (pair_out, atoms_out)


def solution(mesh):
    return jax.shard_map(
        on_device,
        mesh=mesh,
        in_specs=(P("row", "col", None), P(BOTH, None)) + (P(),) * 12,
        out_specs=(P("row", "col", None), P(BOTH, None)),
        check_vma=False,
    )
```

```python
import functools

import jax
import jax.numpy as jnp
from jax import lax
from jax.experimental import pallas as pl
from jax.experimental.pallas import tpu as pltpu
from jax.sharding import PartitionSpec as P

ROWS = 96
COLS = 48
LANES = 128
CHANNELS = 128
TOKENS = 768
QUERIES = 32
KEYS = 128
HALO = 48
ATOM_ROWS = 192
KEY_ROWS = ATOM_ROWS + 2 * HALO
HEADS = 4
HEAD_DIM = 32
NEAR = 5
BAND_ROWS = 16
BAND_COLS = 32
EDGE_ROWS = 72
WIDE = 56
SUM_ROWS = 36
SUM_TILES = CHANNELS * SUM_ROWS // 8
EPSILON = 1e-05
BOTH = ("row", "col")
VMEM_LIMIT = 20 * 1024 * 1024

F32 = jnp.float32
BF16 = jnp.bfloat16


def layer_norm(values):
    center = values - jnp.mean(values, -1, keepdims=True)
    return center * lax.rsqrt(jnp.mean(center * center, -1, keepdims=True) + EPSILON)


def sigmoid(values):
    return 0.5 * jnp.tanh(0.5 * values) + 0.5


def edges_kernel(
    pair_ref,
    gain_ref,
    weight_ref,
    edges_ref,
    gain_out_ref,
    tile_ref,
    gain_in_ref,
    weight_in_ref,
    wide_ref,
    stage_ref,
    ready_ref,
    in_sems,
    param_sems,
    out_sems,
):
    steps = ROWS // 8
    gain_copy = pltpu.make_async_copy(gain_ref, gain_in_ref, param_sems.at[0])
    weight_copy = pltpu.make_async_copy(weight_ref, weight_in_ref, param_sems.at[1])
    tile_copies = [
        pltpu.make_async_copy(
            pair_ref.at[pl.ds(step * 8, 8)], tile_ref.at[pl.ds(step * 8, 8)], in_sems.at[step]
        )
        for step in range(steps)
    ]
    gain_copy.start()
    for copy in tile_copies:
        copy.start()
    weight_copy.start()
    gain_copy.wait()
    gain_out_ref[...] = gain_in_ref[...]
    gain = jnp.broadcast_to(gain_in_ref[...], (2 * LANES, CHANNELS)).T
    same = lax.broadcasted_iota(jnp.int32, (CHANNELS, CHANNELS), 0) == lax.broadcasted_iota(
        jnp.int32, (CHANNELS, CHANNELS), 1
    )
    centering = (same.astype(F32) - 1.0 / CHANNELS).astype(BF16)

    def norm_step(step, carry):
        rows = pl.ds(step * 8, 8)
        pltpu.make_async_copy(pair_ref.at[rows], tile_ref.at[rows], in_sems.at[step]).wait()
        tile = tile_ref[rows].astype(F32)
        for at in range(8):
            start = pl.multiple_of((step * 8 + at) * WIDE, 8)
            wide_ref[pl.ds(start, COLS), :] = tile[at]
        return carry

    lax.fori_loop(0, steps, norm_step, 0, unroll=3)
    weight_copy.wait()
    weight = weight_in_ref[:, :512].T

    def packed(col, third, extra):
        main = wide_ref[pl.ds(col, ROWS, stride=WIDE), :]
        rest = wide_ref[pl.ds(third * 32 * WIDE + extra, 32, stride=WIDE), :]
        return jnp.concatenate([main, rest], 0).astype(BF16)

    def emit(sources, count):
        for at in range(0, count, 2):
            rows = jnp.concatenate([packed(*source) for source in sources[at : at + 2]], 0)
            center = lax.dot_general(
                centering, rows, (((1,), (1,)), ((), ())), preferred_element_type=F32
            )
            scale = lax.rsqrt(jnp.mean(center * center, 0, keepdims=True) + EPSILON)
            inputs = (center * scale * gain).astype(BF16)
            project = jnp.dot(weight, inputs, preferred_element_type=F32)
            left = sigmoid(project[:128]) * project[128:256]
            right = sigmoid(project[256:384]) * project[384:]
            for half in range(2):
                lanes = slice(half * LANES, (half + 1) * LANES)
                stage_ref[pl.ds(at + half, CHANNELS, stride=24), :] = left[:, lanes]
                stage_ref[pl.ds(count + at + half, CHANNELS, stride=24), :] = right[:, lanes]

    def block_copy(group):
        rows = pl.ds(pl.multiple_of(group * 16, 16), 16)
        return pltpu.make_async_copy(
            ready_ref.at[group], edges_ref.at[:, rows, :], out_sems.at[group]
        )

    def block(group, carry):
        sources = []
        for at in range(8):
            third = jnp.where(group < 3, group, at // 4)
            extra = jnp.where(group < 3, 36 + at, 44 + at % 4)
            sources.append((group * 8 + at, third, extra))
        emit(sources, 8)
        ready_ref[group] = stage_ref[: CHANNELS * 24].reshape(CHANNELS, 24, LANES)[:, :16].astype(BF16)
        block_copy(group).start()
        return carry

    lax.fori_loop(0, 4, block, 0, unroll=4)
    emit([(32 + at, 2, 44 + at) for at in range(4)], 4)
    ready_ref[4, :, 0:8, :] = stage_ref[: CHANNELS * 24].reshape(CHANNELS, 24, LANES)[:, :8].astype(BF16)
    last = pltpu.make_async_copy(
        ready_ref.at[4, :, pl.ds(0, 8), :], edges_ref.at[:, pl.ds(64, 8), :], out_sems.at[4]
    )
    last.start()
    for group in range(4):
        block_copy(group).wait()
    last.wait()


def edges(pair, pair_gain, weight):
    far = pl.BlockSpec(memory_space=pltpu.HBM)
    return pl.pallas_call(
        edges_kernel,
        out_shape=(
            jax.ShapeDtypeStruct((CHANNELS, EDGE_ROWS, LANES), BF16),
            jax.ShapeDtypeStruct((1, CHANNELS), F32),
        ),
        in_specs=[far] * 3,
        out_specs=(far, pl.BlockSpec(memory_space=pltpu.VMEM)),
        scratch_shapes=[
            pltpu.VMEM((ROWS, COLS, CHANNELS), BF16),
            pltpu.VMEM((1, CHANNELS), F32),
            pltpu.VMEM((CHANNELS, 640), BF16),
            pltpu.VMEM(((ROWS + 1) * WIDE, CHANNELS), F32),
            pltpu.VMEM(((CHANNELS + 1) * 24, LANES), F32),
            pltpu.VMEM((5, CHANNELS, 16, LANES), BF16),
            pltpu.SemaphoreType.DMA((ROWS // 8,)),
            pltpu.SemaphoreType.DMA((2,)),
            pltpu.SemaphoreType.DMA((5,)),
        ],
        compiler_params=pltpu.CompilerParams(vmem_limit_bytes=56 * 1024 * 1024),
        cost_estimate=pl.CostEstimate(
            flops=2 * ROWS * COLS * 128 * 512, bytes_accessed=4000000, transcendentals=1200000
        ),
        name="edges",
    )(pair, pair_gain, weight)


def triangle_kernel(
    arrived_ref,
    sums_ref,
    chunks_ref,
    left_ref,
    right_ref,
    flip_ref,
    out_ref,
    ready_ref,
    in_sems,
    sems,
):
    def row_load(row):
        part = pl.ds(pl.multiple_of(row * 16, 16), 16)
        return pltpu.make_async_copy(arrived_ref.at[part], chunks_ref.at[part], in_sems.at[row])

    for row in range(8):
        row_load(row).start()

    lane = lax.broadcasted_iota(jnp.int32, (8, LANES), 1)
    low = lax.broadcasted_iota(jnp.int32, (8, LANES), 0) < 4

    def thirds(first, second, third):
        return jnp.where(
            lane < 32,
            pltpu.roll(first, 32, 1),
            jnp.where(lane < 64, pltpu.roll(second, 64, 1), pltpu.roll(third, 96, 1)),
        )

    def gather_row(row, carry):
        row_load(row).wait()
        lanes = pl.ds(pl.multiple_of(row * LANES, LANES), LANES)

        def gather(col, carry):
            chunk = chunks_ref[row * 16 + col].astype(F32)
            part = [chunk[at * 8 : at * 8 + 8] for at in range(9)]
            tail = part[8]
            turned = pltpu.roll(tail, 4, 0)
            at_rows = pl.ds(pl.multiple_of(col * COLS, COLS), COLS)
            left, right = part[0:8:2], part[1:8:2]
            for ref, main, last, spare in (
                (left_ref, left, tail, turned),
                (right_ref, right, turned, tail),
            ):
                fine = thirds(pltpu.roll(main[3], 4, 0), main[3], spare)
                whole = jnp.concatenate(
                    main + [thirds(main[0], main[1], main[2]), jnp.where(low, last, fine)], 0
                )
                ref[at_rows, lanes] = whole.astype(BF16)
            return carry

        lax.fori_loop(0, 16, gather, 0, unroll=16)
        flip_ref[pl.ds(pl.multiple_of(row * ROWS, ROWS), ROWS), :] = right_ref[:, lanes].T[:ROWS]
        return carry

    lax.fori_loop(0, 8, gather_row, 0, unroll=True)

    def row_copy(row):
        part = pl.ds(row * 72, 72)
        return pltpu.make_async_copy(ready_ref.at[part], sums_ref.at[part], sems.at[row])

    for pair_at in range(4):
        lanes = pl.ds(pl.multiple_of(pair_at * 256, 256), 256)
        out_ref[pair_at % 2] = jnp.dot(
            flip_ref[...], left_ref[:, lanes], preferred_element_type=F32
        )
        for half in range(2):
            row = pair_at * 2 + half

            def pack(col_pair, carry):
                tiles = []
                for side in range(2):
                    start = pl.multiple_of(col_pair * ROWS + side * COLS, 16)
                    block = out_ref[
                        pair_at % 2, pl.ds(start, COLS), half * LANES : (half + 1) * LANES
                    ]
                    part = [block[at * 8 : at * 8 + 8] for at in range(6)]
                    turned = pltpu.roll(part[4], 4, 0)
                    fine = jnp.where(low, pltpu.roll(turned, 96, 1), pltpu.roll(part[4], 64, 1))
                    rest = [pltpu.roll(part[5], 96 - 32 * at, 1) for at in range(3)] + [fine]
                    whole = [jnp.where(lane < 96, part[at], rest[at]) for at in range(4)]
                    if side == 0:
                        last = jnp.where(lane < 96, part[4], pltpu.roll(turned, 32, 1))
                        tiles = whole
                    else:
                        other = jnp.where(lane < 96, turned, pltpu.roll(part[4], 32, 1))
                        tiles = tiles + [jnp.where(low, last, other)] + whole
                packed = jnp.concatenate(tiles, 0).reshape(9, 8, LANES).astype(BF16)
                ready_ref[pl.ds((row * 8 + col_pair) * 9, 9)] = packed
                return carry

            lax.fori_loop(0, 8, pack, 0, unroll=8)
            row_copy(row).start()

    for row in range(8):
        row_copy(row).wait()


def triangle(chunks):
    return pl.pallas_call(
        triangle_kernel,
        out_shape=jax.ShapeDtypeStruct((SUM_TILES, 8, LANES), BF16),
        in_specs=[pl.BlockSpec(memory_space=pltpu.HBM)],
        out_specs=pl.BlockSpec(memory_space=pltpu.HBM),
        scratch_shapes=[
            pltpu.VMEM((CHANNELS, EDGE_ROWS, LANES), BF16),
            pltpu.VMEM((TOKENS, 1024), BF16),
            pltpu.VMEM((TOKENS, 1024), BF16),
            pltpu.VMEM((TOKENS, TOKENS), BF16),
            pltpu.VMEM((2, TOKENS, 256), F32),
            pltpu.VMEM((SUM_TILES, 8, LANES), BF16),
            pltpu.SemaphoreType.DMA((8,)),
            pltpu.SemaphoreType.DMA((8,)),
        ],
        compiler_params=pltpu.CompilerParams(vmem_limit_bytes=52 * 1024 * 1024),
        cost_estimate=pl.CostEstimate(
            flops=2 * 1024 * 1024 * 768, bytes_accessed=4000000, transcendentals=0
        ),
        name="triangle",
    )(chunks)


def update_kernel(
    odd_ref,
    sums_ref,
    pair_ref,
    gate_ref,
    gain_ref,
    weight_ref,
    out_ref,
    pair_in_ref,
    gate_in_ref,
    ready_ref,
    normed_ref,
    fold_ref,
    update_ref,
    pair_sems,
    gate_sems,
    out_sems,
):
    parts = [pl.ds(at * 24, 24) for at in range(4)]
    loads = []
    for at, part in enumerate(parts):
        loads.append(
            (
                pltpu.make_async_copy(pair_ref.at[part], pair_in_ref.at[part], pair_sems.at[at]),
                pltpu.make_async_copy(gate_ref.at[part], gate_in_ref.at[part], gate_sems.at[at]),
            )
        )
        for copy in loads[-1]:
            copy.start()
    gain = jnp.broadcast_to(gain_ref[...], (CHANNELS, LANES)).T
    weight = weight_ref[...]

    def tiles(step):
        return sums_ref[step * 72 : step * 72 + 72].astype(F32).reshape(8, 9, 8, LANES)

    def channel_mean(total):
        fold_ref[...] = total.reshape(2 * SUM_ROWS, LANES)
        mean = (fold_ref[0:SUM_ROWS] + fold_ref[SUM_ROWS:]) * (1.0 / CHANNELS)
        fold_ref[0:SUM_ROWS] = mean
        fold_ref[SUM_ROWS:] = mean
        return fold_ref[...].reshape(1, 9, 8, LANES)

    total = jnp.zeros((9, 8, LANES), F32)
    for step in range(8):
        total = total + jnp.sum(tiles(step), 0)
    mean = channel_mean(total)
    total = jnp.zeros((9, 8, LANES), F32)
    for step in range(8):
        center = tiles(step) - mean
        total = total + jnp.sum(center * center, 0)
    scale = lax.rsqrt(channel_mean(total) + EPSILON)
    for step in range(8):
        normed = (tiles(step) - mean) * scale
        normed_ref[step * 576 : step * 576 + 576, :] = normed.reshape(576, LANES)

    turn = odd_ref[0] * 4
    for at in range(SUM_ROWS):
        row = lax.rem(turn + at, SUM_ROWS)
        block = (normed_ref[pl.ds(row, CHANNELS, stride=SUM_ROWS), :] * gain).astype(BF16)
        update = lax.dot_general(
            block, weight, (((0,), (0,)), ((), ())), preferred_element_type=F32
        )
        update_ref[pl.ds(at, ROWS, stride=WIDE), :] = update[:ROWS]
        third, col = (at // 8, 40 + at % 8) if at < 24 else (at // 4 - 6, 36 + at % 4)
        update_ref[pl.ds(third * 32 * WIDE + col, 32, stride=WIDE), :] = update[ROWS:]

    stores = []
    for at, part in enumerate(parts):
        for copy in loads[at]:
            copy.wait()
        for step in range(at * 3, at * 3 + 3):
            rows = pl.ds(step * 8, 8)
            update = update_ref[pl.ds(step * 8 * WIDE, 8 * WIDE), :].reshape(8, WIDE, CHANNELS)[:, :COLS]
            ready_ref[rows] = (
                pair_in_ref[rows].astype(F32) + gate_in_ref[rows] * update
            ).astype(BF16)
        copy = pltpu.make_async_copy(ready_ref.at[part], out_ref.at[part], out_sems.at[at])
        copy.start()
        stores.append(copy)
    for copy in stores:
        copy.wait()


def update_pair(odd, sums, pair, gate, out_gain, tri_out):
    far = pl.BlockSpec(memory_space=pltpu.HBM)
    near = pl.BlockSpec(memory_space=pltpu.VMEM)
    return pl.pallas_call(
        update_kernel,
        out_shape=jax.ShapeDtypeStruct((ROWS, COLS, CHANNELS), BF16),
        in_specs=[pl.BlockSpec(memory_space=pltpu.SMEM), near, far, far, near, near],
        out_specs=far,
        scratch_shapes=[
            pltpu.VMEM((ROWS, COLS, CHANNELS), BF16),
            pltpu.VMEM((ROWS, COLS, CHANNELS), F32),
            pltpu.VMEM((ROWS, COLS, CHANNELS), BF16),
            pltpu.VMEM(((CHANNELS + 1) * SUM_ROWS, LANES), F32),
            pltpu.VMEM((2 * SUM_ROWS, LANES), F32),
            pltpu.VMEM(((ROWS + 1) * WIDE, CHANNELS), F32),
            pltpu.SemaphoreType.DMA((4,)),
            pltpu.SemaphoreType.DMA((4,)),
            pltpu.SemaphoreType.DMA((4,)),
        ],
        compiler_params=pltpu.CompilerParams(vmem_limit_bytes=50 * 1024 * 1024),
        cost_estimate=pl.CostEstimate(
            flops=2 * ROWS * COLS * 128 * 128, bytes_accessed=6000000, transcendentals=5000
        ),
        name="update_pair",
    )(odd, sums, pair, gate, out_gain, tri_out)


def split3(values):
    high = values.astype(BF16)
    rest = values - high.astype(F32)
    middle = rest.astype(BF16)
    low = (rest - middle.astype(F32)).astype(BF16)
    return high, middle, low


def side_kernel(
    first_ref, place_ref, pair_ref, gain_ref, weight_ref, bias_ref, gate_ref, band_ref, table_ref
):
    gain = gain_ref[...]
    weight = weight_ref[:, 512:]
    bias = jnp.concatenate([part.astype(F32) for part in split3(bias_ref[...])], 0).astype(BF16)
    table_ref[...] = jnp.zeros_like(table_ref)

    def norm_step(step, carry):
        tile = pair_ref[pl.ds(step * 8, 8)].astype(F32).reshape(8 * COLS, CHANNELS)
        normed = layer_norm(tile)
        inputs = (normed * gain).astype(BF16)
        gate = sigmoid(jnp.dot(inputs, weight, preferred_element_type=F32))
        gate_ref[pl.ds(step * 8, 8)] = gate.reshape(8, COLS, CHANNELS)
        parts = split3(normed)
        for at in range(8):
            rows = slice(at * COLS, (at + 1) * COLS)
            found = sum(
                lax.dot_general(
                    bias, part[rows], (((1,), (1,)), ((), ())), preferred_element_type=F32
                )
                for part in parts
            )
            found = found[0:8] + found[8:16] + found[16:24]
            for head in range(HEADS):
                table_ref[head, pl.ds(8 + step * 8 + at, 1), 0:COLS] = found[head : head + 1]
        return carry

    lax.fori_loop(0, ROWS // 8, norm_step, 0, unroll=4)

    lane = lax.broadcasted_iota(jnp.int32, (BAND_ROWS, LANES), 1)
    row_base = place_ref[0]
    col_base = place_ref[1]

    def band_step(slot, carry):
        first = first_ref[jnp.bitwise_xor(slot, place_ref[2])]
        start = first - row_base + 8
        total = jnp.zeros((BAND_ROWS, LANES), F32)
        shift = col_base - (first - NEAR)
        for head in range(HEADS):
            rows = table_ref[head, pl.ds(start, BAND_ROWS), :]
            moved = pltpu.roll(rows, lax.rem(shift + head * BAND_COLS + 16 * LANES, LANES), 1)
            col = lane - head * BAND_COLS - shift
            keep = (lane // BAND_COLS == head) & (col >= 0) & (col < COLS)
            total = total + jnp.where(keep, moved, 0.0)
        band_ref[slot] = total
        return carry

    lax.fori_loop(0, 16, band_step, 0, unroll=4)


def side(first, place, pair, pair_gain, gate_weight, bias_wide):
    whole = pl.BlockSpec(memory_space=pltpu.VMEM)
    scalars = pl.BlockSpec(memory_space=pltpu.SMEM)
    return pl.pallas_call(
        side_kernel,
        out_shape=(
            jax.ShapeDtypeStruct((ROWS, COLS, CHANNELS), F32),
            jax.ShapeDtypeStruct((16, BAND_ROWS, LANES), F32),
        ),
        in_specs=[scalars, scalars, whole, whole, whole, whole],
        out_specs=(whole, whole),
        scratch_shapes=[pltpu.VMEM((HEADS, ROWS + 32, LANES), F32)],
        compiler_params=pltpu.CompilerParams(vmem_limit_bytes=VMEM_LIMIT),
        cost_estimate=pl.CostEstimate(
            flops=8 * ROWS * COLS * 128 * 128, bytes_accessed=5000000, transcendentals=600000
        ),
        name="side",
    )(first, place, pair, pair_gain, gate_weight, bias_wide)


def atoms_kernel(
    base_ref,
    atoms_ref,
    before_ref,
    after_ref,
    band0_ref,
    band1_ref,
    band2_ref,
    band3_ref,
    lane_start_ref,
    lane_end_ref,
    sub_start_ref,
    sub_end_ref,
    gain_ref,
    project_ref,
    output_ref,
    trans_gain_ref,
    up_ref,
    down_ref,
    out_ref,
):
    base = base_ref[0]
    own = atoms_ref[...].astype(F32)
    around = jnp.concatenate(
        [before_ref[...].astype(F32), own, after_ref[...].astype(F32)], 0
    )
    inputs = (layer_norm(around) * gain_ref[...]).astype(BF16)
    projected = jnp.dot(inputs, project_ref[...], preferred_element_type=F32)
    query = projected[HALO : HALO + ATOM_ROWS, 0:128].astype(BF16)
    key = projected[:, 128:256].astype(BF16)
    value = projected[:, 256:384].astype(BF16)
    gate = projected[HALO : HALO + ATOM_ROWS, 384:512].astype(BF16).astype(F32)

    query_atom = base + lax.broadcasted_iota(jnp.int32, (ATOM_ROWS, LANES), 0)
    query_hot = (
        ((query_atom >= lane_start_ref[...]) & (query_atom < lane_end_ref[...]))
        .astype(F32)
        .astype(BF16)
    )
    key_atom = base - HALO + lax.broadcasted_iota(jnp.int32, (LANES, KEY_ROWS), 1)
    key_hot = (
        ((key_atom >= sub_start_ref[...]) & (key_atom < sub_end_ref[...])).astype(F32)
    )
    token_head = lax.broadcasted_iota(jnp.int32, (LANES, KEY_ROWS), 0) // BAND_COLS

    band = band0_ref[0] + band1_ref[0] + band2_ref[0] + band3_ref[0]
    band = jnp.concatenate([band, jnp.zeros((LANES - BAND_ROWS, LANES), F32)], 0)
    picked = [
        jnp.dot(query_hot, part, preferred_element_type=F32).astype(BF16) for part in split3(band)
    ]

    window = lax.broadcasted_iota(jnp.int32, (ATOM_ROWS, KEY_ROWS), 0) // QUERIES
    place = lax.broadcasted_iota(jnp.int32, (ATOM_ROWS, KEY_ROWS), 1)
    near = place - window * QUERIES
    atom = base - HALO + place
    allowed = (near >= 0) & (near < KEYS) & (atom >= 0) & (atom < TOKENS * 32)
    lane_head = lax.broadcasted_iota(jnp.int32, (ATOM_ROWS, LANES), 1) // HEAD_DIM
    mixed = jnp.zeros((ATOM_ROWS, LANES), F32)
    for head in range(HEADS):
        own_query = jnp.where(lane_head == head, query.astype(F32), 0.0).astype(BF16)
        scores = lax.dot_general(
            own_query, key, (((1,), (1,)), ((), ())), preferred_element_type=F32
        ) * (HEAD_DIM**-0.5)
        head_hot = jnp.where(token_head == head, key_hot, 0.0).astype(BF16)
        for part in picked:
            scores = scores + jnp.dot(part, head_hot, preferred_element_type=F32)
        scores = jnp.where(allowed, scores, -jnp.inf)
        grown = jnp.exp(scores - jnp.max(scores, -1, keepdims=True))
        weights = (grown / jnp.sum(grown, -1, keepdims=True)).astype(BF16)
        mixed = mixed + jnp.where(
            lane_head == head, jnp.dot(weights, value, preferred_element_type=F32), 0.0
        )
    attended = (mixed * sigmoid(gate)).astype(BF16)
    state = own + jnp.dot(attended, output_ref[...], preferred_element_type=F32)
    inner = (layer_norm(state) * trans_gain_ref[...]).astype(BF16)
    upward = jnp.dot(inner, up_ref[...], preferred_element_type=F32)
    first, second = upward[:, :256], upward[:, 256:]
    hidden = (first * sigmoid(first) * second).astype(BF16)
    out_ref[...] = (
        state + jnp.dot(hidden, down_ref[...], preferred_element_type=F32)
    ).astype(BF16)


def atoms_block(base, *arrays):
    whole = pl.BlockSpec(memory_space=pltpu.VMEM)
    return pl.pallas_call(
        atoms_kernel,
        out_shape=jax.ShapeDtypeStruct((ATOM_ROWS, LANES), BF16),
        in_specs=[pl.BlockSpec(memory_space=pltpu.SMEM)] + [whole] * len(arrays),
        out_specs=whole,
        compiler_params=pltpu.CompilerParams(vmem_limit_bytes=VMEM_LIMIT),
        cost_estimate=pl.CostEstimate(
            flops=2 * 400 * 1000 * 1000, bytes_accessed=2000000, transcendentals=400000
        ),
        name="atoms_block",
    )(base, *arrays)


def on_device(
    pair,
    atoms,
    token_atoms,
    pair_gain,
    tri_proj,
    tri_out,
    out_gain,
    bias_weight,
    atom_gain,
    atom_proj,
    atom_out,
    trans_gain,
    trans_up,
    trans_down,
):
    row_id = lax.axis_index("row")
    col_id = lax.axis_index("col")
    device = row_id * 16 + col_id

    chunks, later_gain = edges(pair, pair_gain[None], tri_proj)
    arrived = lax.all_to_all(chunks, BOTH, 0, 0, tiled=True)

    ends = jnp.cumsum(token_atoms)
    starts = ends - token_atoms
    firsts_at = (row_id * 16 + jnp.arange(16, dtype=jnp.int32)) * ATOM_ROWS
    firsts = jnp.sum((ends[None, :] <= firsts_at[:, None]).astype(jnp.int32), 1)
    first = jnp.sum((ends <= device * ATOM_ROWS).astype(jnp.int32))
    far = jnp.full((LANES,), -1, jnp.int32)
    all_starts = jnp.concatenate([far, starts, far])
    all_ends = jnp.concatenate([far, ends, far])
    lane_start = lax.dynamic_slice(all_starts, (first + LANES,), (LANES,))
    lane_end = lax.dynamic_slice(all_ends, (first + LANES,), (LANES,))
    sub_start = lax.dynamic_slice(all_starts, (first + LANES - NEAR,), (BAND_COLS,))
    sub_end = lax.dynamic_slice(all_ends, (first + LANES - NEAR,), (BAND_COLS,))

    bias_wide = jnp.pad(bias_weight.T, ((0, 4), (0, 0)))
    place = jnp.stack([row_id * ROWS, col_id * COLS, col_id]).astype(jnp.int32)
    gate, bands = side(firsts, place, pair, later_gain, tri_proj, bias_wide)
    def exchange(values, size):
        parts = [values[:size]]
        for at in range(1, 4):
            pairs = [(device, device ^ (at * size)) for device in range(16)]
            parts.append(lax.ppermute(values[at * size : (at + 1) * size], "col", pairs))
        return parts

    halves = exchange(bands, 4)
    ring = list(range(127))
    before = lax.ppermute(atoms[ATOM_ROWS - HALO :], BOTH, [(at, at + 1) for at in ring])
    after = lax.ppermute(atoms[:HALO], BOTH, [(at + 1, at) for at in ring])
    arrived, before, after, *halves = lax.optimization_barrier(
        (arrived, before, after, *halves)
    )
    parts = exchange(sum(halves), 1)
    atoms_out = atoms_block(
        (device * ATOM_ROWS).astype(jnp.int32)[None],
        atoms,
        before,
        after,
        *parts,
        lane_start[None],
        lane_end[None],
        jnp.tile(sub_start, HEADS)[:, None],
        jnp.tile(sub_end, HEADS)[:, None],
        atom_gain[None],
        atom_proj,
        atom_out,
        trans_gain[None],
        trans_up,
        trans_down,
    )

    sums = triangle(arrived)
    chunks = sums.reshape(CHANNELS, SUM_ROWS // 4, 4, LANES)
    returned = lax.all_to_all(chunks, BOTH, 0, 0, tiled=True).reshape(sums.shape)
    odd = lax.rem(col_id, 2).astype(jnp.int32)[None]
    pair_out = update_pair(odd, returned, pair, gate, out_gain[None], tri_out)
    return (pair_out, atoms_out)


def solution(mesh):
    return jax.shard_map(
        on_device,
        mesh=mesh,
        in_specs=(P("row", "col", None), P(BOTH, None)) + (P(),) * 12,
        out_specs=(P("row", "col", None), P(BOTH, None)),
        check_vma=False,
    )
```
